256 devices in a mesh: grp: 4 (over x), dom: 64 (over z, y, core).
Axes of the slice: x: 4, y: 4, z: 8, core: 2. Of those that a mesh axis runs over, the one named last changes fastest.
Arguments:
- fine_nodes: bfloat16 [131072, 128], P(('grp', 'dom')), may hold values from -6 to 6
- cotangent: float32 [131072, 128], P(('grp', 'dom')), may hold values from -6 to 6
- msg_weights: bfloat16 [3, 256, 128], replicated, may hold values from -0.375 to 0.375
- msg_biases: float32 [3, 128], replicated, may hold values from -3 to 3
- node_weights: bfloat16 [3, 256, 128], replicated, may hold values from -0.375 to 0.375
- node_biases: float32 [3, 128], replicated, may hold values from -3 to 3
- node_count: int32 [256], P(('grp', 'dom')), may hold values from 256 to 512, as said below
- fine_edges: int32 [256, 2, 3072], P(('grp', 'dom')), may hold values from 0 to 639, as said below
- fine_send: int32 [256, 2, 64], P(('grp', 'dom')), may hold values from 0 to 255, as said below
- pool_map: int32 [256, 512], P(('grp', 'dom')), may hold values from 0 to 127, as said below
- coarse_edges: int32 [256, 2, 384], P(('grp', 'dom')), may hold values from 0 to 79, as said below
- top_map: int32 [256, 64], P(('grp', 'dom')), may hold values from 0 to 2047, as said below
- top_edges: int32 [2, 12288], replicated, may hold values from 0 to 2047
Outputs:
- fine_out: bfloat16 [131072, 128], P(('grp', 'dom'))
- node_grad: float32 [131072, 128], P(('grp', 'dom'))
- msg_weight_grad: float32 [3, 256, 128], replicated
- msg_bias_grad: float32 [3, 128], replicated
- node_weight_grad: float32 [3, 256, 128], replicated
- node_bias_grad: float32 [3, 128], replicated
The draws below stay inside these ranges and needn't reach their ends.
Inputs may be any that keep to these rules, and one draw needn't show every extreme that they name: `node_count`: some partition has all 512 rows live in every draw. fine_edges[p, 0, e] indexes partition p's fine_ext: a live row of its own, or 512 + r for received row r; fine_edges[p, 1, e] is a live row of partition p. `fine_send`: every listed row is live. `pool_map`: the last partition maps only to its own coarse nodes, below 64. coarse_edges[p, 0, e] indexes partition p's coarse_ext; coarse_edges[p, 1, e] is below 64. `top_map`: the coarse nodes of partition p map only to coarsest nodes (p - 1) * (8) to (p + 2) * 8 - 1, taken modulo 2048; in every partition both ends of that window are used.
All inputs are finite; a program needn't handle non-finite values.
Results may differ from the reference program's by a relative error of at most 0.012.
The reference program's roundings to bfloat16 on the way count: a program that leaves them out, or rounds other values in their place, can miss the bound.
Values may be sent and summed in bfloat16 or wider, within the bound.
A program may use at most 128 MiB of HBM per device.

```python
from functools import partial
import jax
import jax.numpy as jnp
from jax import lax

W = 128
NF = 512
NPART = 256
NODES = 131072
HALO = 64
EF = 3072
NC = 64
HC = 8
EC = 384
NT = 2048
ET = 12288


def live_counts(key):
    base_key = jax.random.fold_in(key, 501)
    counts = jax.random.randint(base_key, (NPART,), NF // 2, NF + 1)
    full_spot = jax.random.randint(jax.random.fold_in(base_key, 1), (), 0, NPART)
    return jnp.where(jnp.arange(NPART) == full_spot, NF, counts).astype(jnp.int32)


def draw_node_count(key, part):
    return live_counts(key)


def draw_fine_edges(key, part):
    counts = live_counts(key)
    key = jax.random.fold_in(key, 11)
    first, second, third, fourth = jax.random.split(key, 4)
    target = jax.random.randint(first, (NPART, EF), 0, counts[:, None])
    local_src = jax.random.randint(second, (NPART, EF), 0, counts[:, None])
    remote = NF + jax.random.randint(third, (NPART, EF), 0, 2 * HALO)
    pick_halo = jax.random.randint(fourth, (NPART, EF), 0, 6)
    source = jnp.where(pick_halo == 0, remote, local_src)
    return jnp.stack([source, target], axis=1).astype(jnp.int32)


def draw_fine_send(key, part):
    key = jax.random.fold_in(key, 12)
    return jax.random.randint(key, (NPART, 2, HALO), 0, NF // 2).astype(jnp.int32)


def draw_pool_map(key, part):
    key = jax.random.fold_in(key, 13)
    slots = jax.random.randint(key, (NPART, NF), 0, 2 * NC)
    last_part = (jnp.arange(NPART) == NPART - 1)[:, None]
    return jnp.where(last_part, slots % NC, slots).astype(jnp.int32)


def draw_coarse_edges(key, part):
    key = jax.random.fold_in(key, 14)
    first, second = jax.random.split(key, 2)
    source = jax.random.randint(first, (NPART, EC), 0, NC + 2 * HC)
    target = jax.random.randint(second, (NPART, EC), 0, NC)
    return jnp.stack([source, target], axis=1).astype(jnp.int32)


def draw_top_map(key, part):
    key = jax.random.fold_in(key, 15)
    first, second, third = jax.random.split(key, 3)
    per_part = NT // NPART
    start_ids = (jnp.arange(NPART)[:, None] - 1) * per_part
    offsets = jax.random.randint(first, (NPART, NC), 0, 3 * per_part)
    low_spot = jax.random.randint(second, (NPART, 1), 0, NC // 2)
    high_spot = NC // 2 + jax.random.randint(third, (NPART, 1), 0, NC // 2)
    column = jnp.arange(NC)[None, :]
    offsets = jnp.where(column == low_spot, 0, jnp.where(column == high_spot, 3 * per_part - 1, offsets))
    return ((start_ids + offsets) % NT).astype(jnp.int32)


def draw_top_edges(key, part):
    key = jax.random.fold_in(key, 16)
    first, second, third = jax.random.split(key, 3)
    per_part = NT // NPART
    target = jax.random.randint(first, (ET,), 0, NT)
    spread = jax.random.randint(second, (ET,), -per_part, per_part + 1)
    opposite = (target + NT // 2 + spread) % NT
    anywhere = jax.random.randint(third, (ET,), 0, NT)
    far_pick = jnp.arange(ET) % 6 < 4
    source = jnp.where(far_pick, opposite, anywhere)
    return jnp.stack([source, target], axis=0).astype(jnp.int32)


def block_scale(own_key, extent, shards, low, top_value):
    loudness, own = 1.0, jax.random.fold_in(own_key, 6)
    for dim, blocks in shards:
        steps = jnp.exp(jax.random.uniform(jax.random.fold_in(own, dim), (blocks,), jnp.float32, low / len(shards), top_value / len(shards)))
        loudness = loudness * jnp.repeat(steps, extent[dim] // blocks).reshape([-1 if axis == dim else 1 for axis in range(len(extent))])
    return loudness


def centred(own_key, shape, deviation, limit, shards=(), dtype=jnp.bfloat16):
    loudness = block_scale(own_key, shape, shards, -0.22, 0.18) if shards else 1.0
    array = jax.random.normal(own_key, shape, jnp.float32) * deviation * loudness
    return jnp.minimum(jnp.maximum(array, -limit), limit).astype(dtype)


def setup_inputs(seed: int = 0) -> dict:
    key_of = jax.random.split(jax.random.key(seed), 14)
    fine_nodes = centred(key_of[0], (NODES, W), 1.0, 6.0, ((0, 256),))
    cotangent = centred(key_of[1], (NODES, W), 1.0, 6.0, ((0, 256),), jnp.float32)
    msg_weights = centred(key_of[2], (3, 2 * W, W), (2 * W) ** -0.5, 0.375)
    msg_biases = centred(key_of[3], (3, W), 0.5, 3.0, (), jnp.float32)
    node_weights = centred(key_of[4], (3, 2 * W, W), (2 * W) ** -0.5, 0.375)
    node_biases = centred(key_of[5], (3, W), 0.5, 3.0, (), jnp.float32)
    node_count = draw_node_count(jax.random.fold_in(key_of[13], 71), 0)
    fine_edges = draw_fine_edges(jax.random.fold_in(key_of[13], 71), 0)
    fine_send = draw_fine_send(jax.random.fold_in(key_of[13], 71), 0)
    pool_map = draw_pool_map(jax.random.fold_in(key_of[13], 71), 0)
    coarse_edges = draw_coarse_edges(jax.random.fold_in(key_of[13], 71), 0)
    top_map = draw_top_map(jax.random.fold_in(key_of[13], 71), 0)
    top_edges = draw_top_edges(jax.random.fold_in(key_of[13], 71), 0)
    return dict(fine_nodes=fine_nodes, cotangent=cotangent, msg_weights=msg_weights, msg_biases=msg_biases, node_weights=node_weights, node_biases=node_biases, node_count=node_count, fine_edges=fine_edges, fine_send=fine_send, pool_map=pool_map, coarse_edges=coarse_edges, top_map=top_map, top_edges=top_edges)


def silu_slope(inputs):
    sigmoid_part = jax.nn.sigmoid(inputs)
    return sigmoid_part * (1.0 + inputs * (1.0 - sigmoid_part))


def block_forward(msg_weight, msg_bias, node_weight, node_bias, node_rows, ext_rows, source, target):
    row_total = node_rows.shape[0]
    edge_pair = jnp.concatenate([jnp.take(ext_rows, source, axis=0), jnp.take(node_rows, target, axis=0)], axis=1)
    pre_act = jnp.dot(edge_pair, msg_weight, preferred_element_type=jnp.float32) + msg_bias
    gathered = jax.ops.segment_sum(jax.nn.silu(pre_act), target, num_segments=row_total).astype(jnp.bfloat16)
    node_pair = jnp.concatenate([node_rows, gathered], axis=1)
    node_act = jnp.dot(node_pair, node_weight, preferred_element_type=jnp.float32) + node_bias
    updated = (node_rows.astype(jnp.float32) + jax.nn.silu(node_act)).astype(jnp.bfloat16)
    return updated, (edge_pair, pre_act, node_pair, node_act)


def block_backward(msg_weight, node_weight, stored, source, target, grad_rows, ext_total):
    edge_pair, pre_act, node_pair, node_act = stored
    row_total = grad_rows.shape[0]
    feature_count = grad_rows.shape[1]
    contract = (((0,), (0,)), ((), ()))
    grad_act = grad_rows * silu_slope(node_act)
    grad_act_low = grad_act.astype(jnp.bfloat16)
    grad_node_weight = lax.dot_general(node_pair, grad_act_low, contract, preferred_element_type=jnp.float32)
    grad_node_bias = jnp.sum(grad_act, axis=0)
    grad_pair = jnp.dot(grad_act_low, node_weight.T, preferred_element_type=jnp.float32)
    grad_nodes = grad_rows + grad_pair[:, :feature_count]
    grad_gathered = grad_pair[:, feature_count:].astype(jnp.bfloat16)
    grad_pre = jnp.take(grad_gathered, target, axis=0).astype(jnp.float32) * silu_slope(pre_act)
    grad_pre_low = grad_pre.astype(jnp.bfloat16)
    grad_msg_weight = lax.dot_general(edge_pair, grad_pre_low, contract, preferred_element_type=jnp.float32)
    grad_msg_bias = jnp.sum(grad_pre, axis=0)
    grad_edges = jnp.dot(grad_pre_low, msg_weight.T, preferred_element_type=jnp.float32)
    grad_ext = jax.ops.segment_sum(grad_edges[:, :feature_count], source, num_segments=ext_total)
    grad_nodes = grad_nodes + jax.ops.segment_sum(grad_edges[:, feature_count:], target, num_segments=row_total)
    return grad_nodes, grad_ext, (grad_msg_weight, grad_msg_bias, grad_node_weight, grad_node_bias)


def from_lower(stacked):
    return jnp.concatenate([jnp.zeros_like(stacked[:1]), stacked[:-1]], axis=0)


def from_upper(stacked):
    return jnp.concatenate([stacked[1:], jnp.zeros_like(stacked[:1])], axis=0)


def take_rows(row_block, index_block):
    return jnp.take(row_block, index_block, axis=0)


def reference(fine_nodes, cotangent, msg_weights, msg_biases, node_weights, node_biases, node_count, fine_edges, fine_send, pool_map, coarse_edges, top_map, top_edges):
    node_rows = fine_nodes.reshape(NPART, NF, W)
    cot_rows = cotangent.reshape(NPART, NF, W)
    alive_mask = (jnp.arange(NF)[None, :] < node_count[:, None]).astype(jnp.float32)
    taken = jax.vmap(take_rows)(node_rows, fine_send)
    from_left = from_lower(taken[:, 1])
    from_right = from_upper(taken[:, 0])
    fine_ext = jnp.concatenate([node_rows, from_left, from_right], axis=1)
    mapped_forward = jax.vmap(block_forward, in_axes=(None, None, None, None, 0, 0, 0, 0))
    fine_hidden, fine_stored = mapped_forward(msg_weights[0], msg_biases[0], node_weights[0], node_biases[0], node_rows, fine_ext, fine_edges[:, 0], fine_edges[:, 1])

    def pool_part(row_block, key_block, mask_block):
        summed = jax.ops.segment_sum(row_block.astype(jnp.float32) * mask_block[:, None], key_block, num_segments=2 * NC)
        counted = jax.ops.segment_sum(mask_block, key_block, num_segments=2 * NC)
        return summed, counted

    pool_sum, pool_count = jax.vmap(pool_part)(fine_hidden, pool_map, alive_mask)
    coarse_sum = pool_sum[:, :NC] + from_lower(pool_sum[:, NC:])
    coarse_den = jnp.maximum(pool_count[:, :NC] + from_lower(pool_count[:, NC:]), 1.0)
    coarse_start = (coarse_sum / coarse_den[:, :, None]).astype(jnp.bfloat16)
    coarse_ext = jnp.concatenate([from_lower(coarse_start[:, NC - HC:]), coarse_start, from_upper(coarse_start[:, :HC])], axis=1)
    coarse_hidden, coarse_stored = mapped_forward(msg_weights[1], msg_biases[1], node_weights[1], node_biases[1], coarse_start, coarse_ext, coarse_edges[:, 0], coarse_edges[:, 1])
    flat_keys = top_map.reshape(-1)
    top_sum = jax.ops.segment_sum(coarse_hidden.reshape(-1, W).astype(jnp.float32), flat_keys, num_segments=NT)
    top_count = jax.ops.segment_sum(jnp.ones((NPART * NC,), jnp.float32), flat_keys, num_segments=NT)
    top_den = jnp.maximum(top_count, 1.0)
    top_start = (top_sum / top_den[:, None]).astype(jnp.bfloat16)
    top_hidden, top_stored = block_forward(msg_weights[2], msg_biases[2], node_weights[2], node_biases[2], top_start, top_start, top_edges[0], top_edges[1])
    coarse_final = (coarse_hidden.astype(jnp.float32) + jnp.take(top_hidden, top_map, axis=0).astype(jnp.float32)).astype(jnp.bfloat16)
    lift_rows = jnp.concatenate([coarse_final, from_upper(coarse_final)], axis=1)
    lifted = jax.vmap(take_rows)(lift_rows, pool_map)
    fine_out = ((fine_hidden.astype(jnp.float32) + lifted.astype(jnp.float32)) * alive_mask[:, :, None]).astype(jnp.bfloat16)

    grad_out = cot_rows * alive_mask[:, :, None]
    grad_lift = jax.vmap(lambda row_block, key_block: jax.ops.segment_sum(row_block, key_block, num_segments=2 * NC))(grad_out, pool_map)
    grad_coarse = grad_lift[:, :NC] + from_lower(grad_lift[:, NC:])
    top_grad = jax.ops.segment_sum(grad_coarse.reshape(-1, W), flat_keys, num_segments=NT)
    grad_top_nodes, grad_top_ext, top_grads = block_backward(msg_weights[2], node_weights[2], top_stored, top_edges[0], top_edges[1], top_grad, NT)
    grad_top_sum = (grad_top_nodes + grad_top_ext) / top_den[:, None]
    grad_coarse = grad_coarse + jnp.take(grad_top_sum, top_map, axis=0)
    coarse_backward = jax.vmap(partial(block_backward, ext_total=NC + 2 * HC), in_axes=(None, None, 0, 0, 0, 0))
    grad_cnodes, grad_cext, coarse_grads = coarse_backward(msg_weights[1], node_weights[1], coarse_stored, coarse_edges[:, 0], coarse_edges[:, 1], grad_coarse)
    grad_start = grad_cnodes + grad_cext[:, HC:HC + NC]
    grad_start = grad_start.at[:, :HC].add(from_lower(grad_cext[:, HC + NC:]))
    grad_start = grad_start.at[:, NC - HC:].add(from_upper(grad_cext[:, :HC]))
    grad_csum = grad_start / coarse_den[:, :, None]
    grad_pool = jnp.concatenate([grad_csum, from_upper(grad_csum)], axis=1)
    grad_fine = grad_out + jax.vmap(take_rows)(grad_pool, pool_map) * alive_mask[:, :, None]
    fine_backward = jax.vmap(partial(block_backward, ext_total=NF + 2 * HALO), in_axes=(None, None, 0, 0, 0, 0))
    grad_fnodes, grad_fext, fine_grads = fine_backward(msg_weights[0], node_weights[0], fine_stored, fine_edges[:, 0], fine_edges[:, 1], grad_fine)
    node_grad = grad_fnodes + grad_fext[:, :NF]
    first_back = from_lower(grad_fext[:, NF + HALO:])
    second_back = from_upper(grad_fext[:, NF:NF + HALO])
    sent_grad = jnp.concatenate([first_back, second_back], axis=1)
    node_grad = node_grad + jax.vmap(lambda row_block, send_block: jax.ops.segment_sum(row_block, send_block.reshape(-1), num_segments=NF))(sent_grad, fine_send)
    grad_scale = 1.0 / (NODES ** 0.5)
    results = [jnp.stack([jnp.sum(fine_grads[member], axis=0), jnp.sum(coarse_grads[member], axis=0), top_grads[member]]) * grad_scale for member in range(4)]
    return (fine_out.reshape(NODES, W), node_grad.reshape(NODES, W), results[0], results[1], results[2], results[3])
```

```python
import functools

import jax
import jax.numpy as jnp
from jax import lax
from jax.experimental import pallas as pl
from jax.experimental.pallas import tpu as pltpu
from jax.sharding import PartitionSpec as P

BF, F32, I32 = jnp.bfloat16, jnp.float32, jnp.int32
MESH = pl.DeviceIdType.MESH
W = 128
TILE = 128
CAP = 128
DOM_SPLIT = (8, 4, 2)
ROWS = 8


def shifted(value, axis, by):
    peers = lax.axis_size(axis)
    pairs = [(i, i + by) for i in range(peers) if 0 <= i + by < peers]
    return lax.ppermute(value, axis, pairs)


def with_halo(cells, sides, width):
    for axis, dim in sides:
        count = lax.axis_size(axis)
        ends = count - 1
        head = lax.slice_in_dim(cells, 0, width, axis=dim)
        tail = lax.slice_in_dim(cells, cells.shape[dim] - width, cells.shape[dim], axis=dim)
        cells = jnp.concatenate(
            [
                lax.ppermute(tail, axis, [(i, (i + 1) % count) for i in range(ends)]),
                cells,
                lax.ppermute(head, axis, [((i + 1) % count, i) for i in range(ends)]),
            ],
            axis=dim,
        )
    return cells


def silu_slope(inputs):
    sigmoid_part = jax.nn.sigmoid(inputs)
    return sigmoid_part * (1.0 + inputs * (1.0 - sigmoid_part))


def block_forward(
    msg_weight, msg_bias, node_weight, node_bias, node_rows, ext_rows, source, target
):
    row_total = node_rows.shape[0]
    edge_pair = jnp.concatenate(
        [jnp.take(ext_rows, source, axis=0), jnp.take(node_rows, target, axis=0)], axis=1
    )
    pre_act = jnp.dot(edge_pair, msg_weight, preferred_element_type=jnp.float32) + msg_bias
    gathered = jax.ops.segment_sum(jax.nn.silu(pre_act), target, num_segments=row_total).astype(
        jnp.bfloat16
    )
    node_pair = jnp.concatenate([node_rows, gathered], axis=1)
    node_act = jnp.dot(node_pair, node_weight, preferred_element_type=jnp.float32) + node_bias
    updated = (node_rows.astype(jnp.float32) + jax.nn.silu(node_act)).astype(jnp.bfloat16)
    return (updated, (edge_pair, pre_act, node_pair, node_act))


def block_backward(msg_weight, node_weight, stored, source, target, grad_rows, ext_total):
    edge_pair, pre_act, node_pair, node_act = stored
    row_total = grad_rows.shape[0]
    feature_count = grad_rows.shape[1]
    contract = (((0,), (0,)), ((), ()))
    grad_act = grad_rows * silu_slope(node_act)
    grad_act_low = grad_act.astype(jnp.bfloat16)
    grad_node_weight = lax.dot_general(
        node_pair, grad_act_low, contract, preferred_element_type=jnp.float32
    )
    grad_node_bias = jnp.sum(grad_act, axis=0)
    grad_pair = jnp.dot(grad_act_low, node_weight.T, preferred_element_type=jnp.float32)
    grad_nodes = grad_rows + grad_pair[:, :feature_count]
    grad_gathered = grad_pair[:, feature_count:].astype(jnp.bfloat16)
    grad_pre = jnp.take(grad_gathered, target, axis=0).astype(jnp.float32) * silu_slope(pre_act)
    grad_pre_low = grad_pre.astype(jnp.bfloat16)
    grad_msg_weight = lax.dot_general(
        edge_pair, grad_pre_low, contract, preferred_element_type=jnp.float32
    )
    grad_msg_bias = jnp.sum(grad_pre, axis=0)
    grad_edges = jnp.dot(grad_pre_low, msg_weight.T, preferred_element_type=jnp.float32)
    grad_ext = jax.ops.segment_sum(grad_edges[:, :feature_count], source, num_segments=ext_total)
    grad_nodes = grad_nodes + jax.ops.segment_sum(
        grad_edges[:, feature_count:], target, num_segments=row_total
    )
    return (
        grad_nodes,
        grad_ext,
        (grad_msg_weight, grad_msg_bias, grad_node_weight, grad_node_bias),
    )


def any_lists(
    fine_nodes,
    cotangent,
    msg_weights,
    msg_biases,
    node_weights,
    node_biases,
    node_count,
    fine_edges,
    fine_send,
    pool_map,
    coarse_edges,
    top_map,
    top_edges,
):
    fine_total = fine_nodes.shape[0]
    halo_rows = fine_send.shape[2]
    coarse_total = fine_total // 8
    coarse_rim = coarse_total // 8
    part_total = lax.axis_size(("grp", "dom"))
    top_total = fine_total * part_total // 64
    alive_mask = (jnp.arange(fine_total) < node_count[0]).astype(jnp.float32)
    send_rows = fine_send[0]
    pool_keys = pool_map[0]
    top_keys = top_map[0]
    from_left = shifted(jnp.take(fine_nodes, send_rows[1], axis=0), ("grp", "dom"), 1)
    from_right = shifted(jnp.take(fine_nodes, send_rows[0], axis=0), ("grp", "dom"), -1)
    fine_ext = jnp.concatenate([fine_nodes, from_left, from_right], axis=0)
    fine_hidden, fine_stored = block_forward(
        msg_weights[0],
        msg_biases[0],
        node_weights[0],
        node_biases[0],
        fine_nodes,
        fine_ext,
        fine_edges[0, 0],
        fine_edges[0, 1],
    )
    pool_table = (pool_keys[None, :] == jnp.arange(2 * coarse_total)[:, None]).astype(
        jnp.float32
    ) * alive_mask[None, :]
    pool_sum = jnp.dot(
        pool_table.astype(jnp.bfloat16), fine_hidden, preferred_element_type=jnp.float32
    )
    pool_count = jnp.sum(pool_table, axis=1)
    lower_sum, lower_count = shifted(
        (pool_sum[coarse_total:], pool_count[coarse_total:]), ("grp", "dom"), 1
    )
    coarse_den = jnp.maximum(pool_count[:coarse_total] + lower_count, 1.0)
    coarse_start = ((pool_sum[:coarse_total] + lower_sum) / coarse_den[:, None]).astype(
        jnp.bfloat16
    )
    coarse_ext = with_halo(coarse_start, ((("grp", "dom"), 0),), coarse_rim)
    coarse_hidden, coarse_stored = block_forward(
        msg_weights[1],
        msg_biases[1],
        node_weights[1],
        node_biases[1],
        coarse_start,
        coarse_ext,
        coarse_edges[0, 0],
        coarse_edges[0, 1],
    )
    local_top = jax.ops.segment_sum(
        coarse_hidden.astype(jnp.float32), top_keys, num_segments=top_total
    )
    local_count = jax.ops.segment_sum(
        jnp.ones((coarse_total,), jnp.float32), top_keys, num_segments=top_total
    )
    top_sum, top_count = lax.psum((local_top, local_count), ("grp", "dom"))
    top_den = jnp.maximum(top_count, 1.0)
    top_start = (top_sum / top_den[:, None]).astype(jnp.bfloat16)
    top_hidden, top_stored = block_forward(
        msg_weights[2],
        msg_biases[2],
        node_weights[2],
        node_biases[2],
        top_start,
        top_start,
        top_edges[0],
        top_edges[1],
    )
    coarse_final = (
        coarse_hidden.astype(jnp.float32)
        + jnp.take(top_hidden, top_keys, axis=0).astype(jnp.float32)
    ).astype(jnp.bfloat16)
    upper_rows = shifted(coarse_final, ("grp", "dom"), -1)
    lifted = jnp.take(jnp.concatenate([coarse_final, upper_rows], axis=0), pool_keys, axis=0)
    fine_out = (
        (fine_hidden.astype(jnp.float32) + lifted.astype(jnp.float32)) * alive_mask[:, None]
    ).astype(jnp.bfloat16)
    grad_out = cotangent * alive_mask[:, None]
    grad_lift = jnp.dot(
        pool_table, grad_out, precision=lax.Precision.HIGHEST, preferred_element_type=jnp.float32
    )
    lower_grad = shifted(grad_lift[coarse_total:], ("grp", "dom"), 1)
    grad_coarse = grad_lift[:coarse_total] + lower_grad
    top_local = jax.ops.segment_sum(grad_coarse, top_keys, num_segments=top_total)
    top_grad = lax.psum(top_local, ("grp", "dom"))
    grad_top_nodes, grad_top_ext, top_grads = block_backward(
        msg_weights[2], node_weights[2], top_stored, top_edges[0], top_edges[1], top_grad, top_total
    )
    grad_top_sum = (grad_top_nodes + grad_top_ext) / top_den[:, None]
    grad_coarse = grad_coarse + jnp.take(grad_top_sum, top_keys, axis=0)
    grad_cnodes, grad_cext, coarse_grads = block_backward(
        msg_weights[1],
        node_weights[1],
        coarse_stored,
        coarse_edges[0, 0],
        coarse_edges[0, 1],
        grad_coarse,
        coarse_total + 2 * coarse_rim,
    )
    grad_start = grad_cnodes + grad_cext[coarse_rim : coarse_rim + coarse_total]
    rim_pair = jnp.concatenate(
        [grad_cext[:coarse_rim], grad_cext[coarse_rim + coarse_total :]], axis=0
    )
    returned = with_halo(rim_pair, ((("grp", "dom"), 0),), coarse_rim)
    grad_start = grad_start.at[:coarse_rim].add(returned[:coarse_rim])
    grad_start = grad_start.at[coarse_total - coarse_rim :].add(returned[3 * coarse_rim :])
    grad_csum = grad_start / coarse_den[:, None]
    upper_grad = shifted(grad_csum.astype(jnp.bfloat16), ("grp", "dom"), -1).astype(grad_csum.dtype)
    grad_pool = jnp.concatenate([grad_csum, upper_grad], axis=0)
    grad_fine = grad_out + jnp.take(grad_pool, pool_keys, axis=0) * alive_mask[:, None]
    grad_fnodes, grad_fext, fine_grads = block_backward(
        msg_weights[0],
        node_weights[0],
        fine_stored,
        fine_edges[0, 0],
        fine_edges[0, 1],
        grad_fine,
        fine_total + 2 * halo_rows,
    )
    node_grad = grad_fnodes + grad_fext[:fine_total]
    left_grad = grad_fext[fine_total : fine_total + halo_rows]
    right_grad = grad_fext[fine_total + halo_rows :]
    first_back = shifted(right_grad.astype(jnp.bfloat16), ("grp", "dom"), 1).astype(
        right_grad.dtype
    )
    second_back = shifted(left_grad.astype(jnp.bfloat16), ("grp", "dom"), -1).astype(
        left_grad.dtype
    )
    sent_grad = jnp.concatenate([first_back, second_back], axis=0)
    node_grad = node_grad + jax.ops.segment_sum(
        sent_grad, send_rows.reshape(-1), num_segments=fine_total
    )
    summed = lax.psum(
        (
            jnp.stack([fine_grads[0], coarse_grads[0]]),
            jnp.stack([fine_grads[1], coarse_grads[1]]),
            jnp.stack([fine_grads[2], coarse_grads[2]]),
            jnp.stack([fine_grads[3], coarse_grads[3]]),
        ),
        ("grp", "dom"),
    )
    grad_scale = 1.0 / (fine_total * part_total) ** 0.5
    results = [
        jnp.concatenate([summed[member], top_grads[member][None]], axis=0) * grad_scale
        for member in range(4)
    ]
    return (fine_out, node_grad, results[0], results[1], results[2], results[3])


def mm(a, b):
    return jnp.dot(a, b, preferred_element_type=F32)


def nt(a, b):
    return lax.dot_general(a, b, (((1,), (1,)), ((), ())), preferred_element_type=F32)


def tn(a, b):
    return lax.dot_general(a, b, (((0,), (0,)), ((), ())), preferred_element_type=F32)


def wide(v):
    high = v.astype(BF)
    return jnp.concatenate([high, (v - high.astype(F32)).astype(BF)], axis=1)


def fold(v):
    return v[:, :W] + v[:, W:]


def nt_split(v, weight):
    high = v.astype(BF)
    return nt(high, weight) + nt((v - high.astype(F32)).astype(BF), weight)


def iota(shape, dim):
    return lax.broadcasted_iota(I32, shape, dim)


def hot(mask):
    return jnp.where(mask, 1.0, 0.0).astype(BF)


def down_lanes(row):
    return jnp.transpose(jnp.broadcast_to(row, (TILE, TILE)))


def sigmoid(v):
    return 0.5 * jnp.tanh(0.5 * v) + 0.5


def pad_rows(v, total=TILE):
    return jnp.concatenate([v, jnp.zeros((total - v.shape[0], v.shape[1]), v.dtype)], axis=0)


def sum_slots(ref, count):
    total = ref[0]
    for slot in range(1, count):
        total = total + ref[slot]
    return total


def step_kernel(
    sizes,
    x_ref, cot_ref, mw_ref, mb_ref, nw_ref, nb_ref, cnt_ref, idx_ref, te_ref,
    out_ref, ngrad_ref, mwg_ref, mbg_ref, nwg_ref, nbg_ref,
    gat, sca, hl, slope, msgs, act_slope, hidden, aggf, pool_t, pool_l,
    gcat, gcat_t, o_top, l_top, pos_s, key_s,
    sendbuf, halo, e0s, e0r, e1s, e1r, pss, psr, rims, rimr, tss, tsr,
    cb1, yb1, tab1, cb2, yb2, tab2, ths, thr, cfs, cfr, gts, gtr, rgs, rgr, ugs, ugr, bgs, bgr,
    f_cs, f_cr, f_xs, f_xr, f_zs, f_zr, f_yr, f_g,
    a_cs, a_cr, a_xs, a_xr, a_zs, a_zr, a_yr, a_g,
    ssem, rsem,
):
    X, Z, Y, C, nf, ne, nc, nec, nrow = sizes
    DOM = Z * Y * C
    NP = X * DOM
    halo_n = 64
    ext_n = nf + 2 * halo_n
    rim = nc // 8
    gx = lax.axis_index("grp")
    dm = lax.axis_index("dom")
    p = gx * DOM + dm
    z = lax.div(dm, Y * C)
    y = lax.rem(lax.div(dm, C), Y)
    c = lax.rem(dm, C)
    xz = gx * Z + z
    up = lax.rem(p + 1, NP)
    dn = lax.rem(p + NP - 1, NP)
    has_dn = p > 0
    has_up = p < NP - 1
    up_dev = (lax.div(up, DOM), lax.rem(up, DOM))
    dn_dev = (lax.div(dn, DOM), lax.rem(dn, DOM))
    core_dev = (gx, dm + 1 - 2 * c)
    x_devs = [(lax.rem(gx + d, X), dm) for d in range(1, X)]
    z_devs = [(gx, lax.rem(z + d, Z) * (Y * C) + y * C + c) for d in range(1, Z)]
    y_devs = [(gx, z * (Y * C) + lax.rem(y + d, Y) * C + c) for d in range(1, Y)]

    barrier = pltpu.get_barrier_semaphore()
    partners = [up_dev, dn_dev, core_dev] + x_devs + z_devs + y_devs
    for dev in partners:
        pl.semaphore_signal(barrier, inc=1, device_id=dev, device_id_type=MESH)

    started = []

    def send(src, dst, dev):
        spot = len(started)
        copy = pltpu.make_async_remote_copy(
            src_ref=src, dst_ref=dst, send_sem=ssem.at[spot], recv_sem=rsem.at[spot],
            device_id=dev, device_id_type=MESH,
        )
        copy.start()
        started.append(copy)
        return copy

    def arrived(copies):
        for copy in copies:
            copy.wait_recv()

    def row(k, n=1):
        return idx_ref[k : k + n, :]

    ntile = ne // TILE
    ctile = nec // TILE
    base_c = 2 * ntile
    base_s = base_c + 2 * ctile
    base_p = base_s + 1
    base_t = base_p + nf // TILE
    lane = iota((TILE, TILE), 1)
    sub = iota((TILE, TILE), 0)
    ones = jnp.ones((TILE, TILE), BF)

    send_lanes = down_lanes(row(base_s))
    picks = jnp.concatenate([hot(send_lanes == lane + g * TILE) for g in range(nf // TILE)], axis=1)
    sendbuf[...] = mm(picks, x_ref[...]).astype(BF)
    pl.semaphore_wait(barrier, len(partners))
    halo_in = [
        send(sendbuf.at[halo_n : 2 * halo_n], halo.at[0:halo_n], up_dev),
        send(sendbuf.at[0:halo_n], halo.at[halo_n : 2 * halo_n], dn_dev),
    ]

    live = cnt_ref[0]
    alive = jnp.where(iota((nf, W), 0) < live, 1.0, 0.0)
    for g in range(nf // TILE):
        keys = row(base_p + g)
        pool_t[:, g * TILE : (g + 1) * TILE] = hot((sub == keys) & (lane + g * TILE < live))
        pool_l[g * TILE : (g + 1) * TILE, :] = hot((down_lanes(keys) == lane) & (sub + g * TILE < live))
    gout = cot_ref[...] * alive
    counts = mm(pool_t[...], jnp.ones((nf, W), BF))
    lift = fold(mm(pool_t[...], wide(gout)))
    e0s[0:nc, :] = lift[nc:]
    e0s[nc : 2 * nc, :] = counts[nc:]
    e0_in = [send(e0s, e0r, up_dev)]
    rel = row(base_t)
    top_t = hot(sub == rel)
    top_l = hot(down_lanes(rel) == lane)
    top_counts = mm(top_t, ones)

    def build(k, carry):
        src = idx_ref[pl.ds(k, 1), :]
        tgt = idx_ref[pl.ds(ntile + k, 1), :]
        src_lanes, tgt_lanes = down_lanes(src), down_lanes(tgt)
        at = pl.ds(pl.multiple_of(k * TILE, TILE), TILE)
        for g in range(ext_n // TILE):
            gat[at, g * TILE : (g + 1) * TILE] = hot(src_lanes == lane + g * TILE)
            sca[g * TILE : (g + 1) * TILE, at] = hot(sub + g * TILE == src)
        for g in range(nf // TILE):
            gat[at, ext_n + g * TILE : ext_n + (g + 1) * TILE] = hot(tgt_lanes == lane + g * TILE)
            sca[ext_n + g * TILE : ext_n + (g + 1) * TILE, at] = hot(sub + g * TILE == tgt)
        return carry

    lax.fori_loop(0, ntile, build, 0)
    ws0, wt0 = mw_ref[0, :W, :], mw_ref[0, W:, :]
    hl[0:nf, :] = wide(mm(x_ref[...], ws0))
    hl[ext_n : ext_n + nf, :] = wide(mm(x_ref[...], wt0) + mb_ref[0:1, :])

    for k in range(ctile):
        src, tgt = row(base_c + k), row(base_c + ctile + k)
        gcat[k * TILE : (k + 1) * TILE, 0:TILE] = hot(down_lanes(src) == lane)
        gcat[k * TILE : (k + 1) * TILE, TILE:] = hot(down_lanes(tgt) == lane)
        gcat_t[0:TILE, k * TILE : (k + 1) * TILE] = hot(sub == src)
        gcat_t[TILE:, k * TILE : (k + 1) * TILE] = hot(sub == tgt)

    first = p * ROWS
    upper_ones = hot(sub <= lane)
    lower_ones = hot(lane < sub)
    src_e, tgt_e = te_ref[0:TILE, :], te_ref[TILE:, :]
    key_s[...] = (src_e * 2048 + tgt_e + 1).astype(F32)
    block = Y * 2 * ROWS
    half = Y * ROWS
    lists = []
    for values in (tgt_e, src_e):
        mine = (values >= first) & (values < first + ROWS)
        flags = hot(mine)
        offset = mm(lower_ones, mm(flags, ones).astype(BF))
        pos_s[...] = jnp.where(mine, mm(flags, upper_ones) + offset - 1.0, -1.0)
        sub_f = sub.astype(F32)

        def pick(r, acc):
            at = pl.ds(pl.multiple_of(r * 8, 8), 8)
            places, keys8 = pos_s[at, :], key_s[at, :]
            for i in range(8):
                acc = acc + jnp.where(places[i : i + 1, :] == sub_f, keys8[i : i + 1, :], 0.0)
            return acc

        acc = lax.fori_loop(0, -(-nrow // 8), pick, jnp.zeros((TILE, TILE), F32))
        key = jnp.broadcast_to(jnp.sum(acc, axis=1, keepdims=True), (TILE, TILE))
        lists.append((key, jnp.transpose(key)))

    def ends(key):
        code = key.astype(I32) - 1
        empty = code < 0
        src, tgt = lax.shift_right_logical(code, 11), code & 2047
        return jnp.where(empty, -1, src), jnp.where(empty, -1, tgt)

    def place(node):
        inner = lax.rem(node, block)
        spot = lax.div(inner, half) * (X * Z * half) + lax.div(node, block) * half + lax.rem(inner, half)
        return jnp.where(node < 0, -1, spot)

    (t_src, t_tgt), (s_src, s_tgt) = ends(lists[0][0]), ends(lists[1][0])
    t_far, s_far = place(t_src), place(s_tgt)
    for g in range(NP * ROWS // TILE):
        o_top[0:TILE, g * TILE : (g + 1) * TILE] = hot(t_far == lane + g * TILE)
        o_top[TILE:, g * TILE : (g + 1) * TILE] = hot(s_far == lane + g * TILE)
    near = jnp.where(lane < ROWS, lane + first, -2)
    l_top[0:TILE, :] = hot(t_tgt == near)
    l_top[TILE:, :] = hot(s_src == near)
    near_t = jnp.where(sub < ROWS, sub + first, -2)
    t_scat = hot(ends(lists[0][1])[1] == near_t)
    s_scat = hot(ends(lists[1][1])[0] == near_t)

    arrived(e0_in)
    lower = jnp.where(has_dn, e0r[...], 0.0)
    grad_coarse0 = lift[:nc] + lower[:nc]
    den = jnp.maximum(counts[:nc] + lower[nc:], 1.0)
    top_g = fold(mm(top_t, pad_rows(wide(grad_coarse0))))
    e1s[0, 0:ROWS, :] = top_counts[0:ROWS]
    e1s[0, ROWS:, :] = top_g[0:ROWS]
    e1s[1, 0:ROWS, :] = top_counts[2 * ROWS : 3 * ROWS]
    e1s[1, ROWS:, :] = top_g[2 * ROWS : 3 * ROWS]
    e1_in = [send(e1s.at[0], e1r.at[0], dn_dev), send(e1s.at[1], e1r.at[1], up_dev)]

    arrived(halo_in)
    halo_rows = sub
    live_halo = (has_dn & (halo_rows < halo_n)) | (has_up & (halo_rows >= halo_n))
    halo_f = jnp.where(live_halo, halo[...].astype(F32), 0.0).astype(BF)
    hl[nf:ext_n, :] = wide(mm(halo_f, ws0))
    step = 4 * TILE

    def forward(k, carry):
        at = pl.ds(pl.multiple_of(k * step, step), step)
        pre = fold(mm(gat[at, :], hl[...]))
        s = sigmoid(pre)
        slope[at, :] = s * (1.0 + pre * (1.0 - s))
        msgs[at, :] = wide(pre * s)
        return carry

    lax.fori_loop(0, ne // step, forward, 0)

    def node_forward(rows, agg, level):
        act = mm(rows, nw_ref[level, :W, :]) + mm(agg, nw_ref[level, W:, :]) + nb_ref[level : level + 1, :]
        s = sigmoid(act)
        return (rows.astype(F32) + act * s).astype(BF), s * (1.0 + act * (1.0 - s))

    def node_backward(rows, agg, act_slopes, grad, level):
        g_act = grad * act_slopes
        low = g_act.astype(BF)
        pair = nt(low, nw_ref[level])
        return (
            grad + pair[:, :W],
            pair[:, W:].astype(BF),
            tn(rows, low),
            tn(agg, low),
            jnp.sum(g_act, axis=0, keepdims=True),
        )

    for k in range(nf // step):
        at = slice(k * step, (k + 1) * step)
        agg = fold(mm(sca[ext_n + k * step : ext_n + (k + 1) * step, :], msgs[...])).astype(BF)
        new, act_s = node_forward(x_ref[at, :], agg, 0)
        aggf[at, :] = agg
        hidden[at, :] = new
        act_slope[at, :] = act_s

    pooled = mm(pool_t[...], hidden[...])
    pss[...] = pooled[nc:]
    ps_in = [send(pss, psr, up_dev)]
    arrived(e1_in)
    own_win = slice(ROWS, 2 * ROWS)
    top_den = jnp.maximum(top_counts[own_win] + e1r[0, 0:ROWS, :] + e1r[1, 0:ROWS, :], 1.0)
    top_grad = pad_rows(top_g[own_win] + e1r[0, ROWS:, :] + e1r[1, ROWS:, :])
    arrived(ps_in)
    start = ((pooled[:nc] + jnp.where(has_dn, psr[...], 0.0)) / den).astype(BF)
    start_f = start.astype(F32)
    rims[0] = start_f[:rim]
    rims[1] = start_f[nc - rim :]
    rim_in = [send(rims.at[0], rimr.at[0], dn_dev), send(rims.at[1], rimr.at[1], up_dev)]
    start_p = pad_rows(start)
    ws1, wt1 = mw_ref[1, :W, :], mw_ref[1, W:, :]
    near_part = wide(mm(start_p, wt1) + mb_ref[1:2, :])
    arrived(rim_in)
    cext = pad_rows(
        jnp.concatenate(
            [jnp.where(has_dn, rimr[1], 0.0), start_f, jnp.where(has_up, rimr[0], 0.0)], axis=0
        )
    ).astype(BF)
    pre = fold(mm(gcat[...], jnp.concatenate([wide(mm(cext, ws1)), near_part], axis=0)))
    s = sigmoid(pre)
    slope_c = s * (1.0 + pre * (1.0 - s))
    agg_c = fold(mm(gcat_t[TILE:, :], wide(pre * s))).astype(BF)
    c_hidden, act_slope_c = node_forward(start_p, agg_c, 1)
    keep = sub < nc
    c_hidden_f = jnp.where(keep, c_hidden.astype(F32), 0.0)
    top_part = mm(top_t, c_hidden_f.astype(BF))
    tss[0] = top_part[0:ROWS]
    tss[1] = top_part[2 * ROWS : 3 * ROWS]
    ts_in = [send(tss.at[0], tsr.at[0], dn_dev), send(tss.at[1], tsr.at[1], up_dev)]
    arrived(ts_in)
    top_start = ((top_part[own_win] + tsr[0] + tsr[1]) / top_den).astype(BF)

    def gather(own, cb, yb, tab):
        spot = pl.ds(pl.multiple_of(c * ROWS, ROWS), ROWS)
        cb[spot, :] = own
        copies = [send(cb.at[spot], cb.at[spot], core_dev)]
        yield
        arrived(copies)
        yb[y] = cb[...].astype(BF)
        copies = [send(yb.at[y], yb.at[y], dev) for dev in y_devs]
        yield
        arrived(copies)
        part = yb[pl.ds(c * (Y // 2), Y // 2)]
        tab[c, xz] = part.reshape(half, W)
        copies = [send(tab.at[c, xz], tab.at[c, xz], dev) for dev in z_devs]
        yield
        arrived(copies)
        mine = pl.ds(gx * Z, Z)
        copies = [send(tab.at[c, mine], tab.at[c, mine], dev) for dev in x_devs]
        yield
        arrived(copies)
        copies = [send(tab.at[c], tab.at[c], core_dev)]
        yield
        arrived(copies)

    for _ in gather(top_start.astype(F32), cb1, yb1, tab1):
        pass

    ws2, wt2, mb2 = mw_ref[2, :W, :], mw_ref[2, W:, :], mb_ref[2:3, :]
    top_rows = pad_rows(top_start.astype(F32)).astype(BF)
    far = mm(o_top[...], tab1[...].reshape(NP * ROWS, W)).astype(BF)
    close = mm(l_top[...], top_rows).astype(BF)
    t_far_rows, s_far_rows = far[:TILE], far[TILE:]
    t_close_rows, s_close_rows = close[:TILE], close[TILE:]
    pre_t = mm(t_far_rows, ws2) + mm(t_close_rows, wt2) + mb2
    s = sigmoid(pre_t)
    slope_t = s * (1.0 + pre_t * (1.0 - s))
    agg_t = fold(mm(t_scat, wide(pre_t * s))).astype(BF)
    t_hidden, act_slope_t = node_forward(top_rows, agg_t, 2)
    g_nodes, g_agg, dwn2_a, dwn2_b, dbn2 = node_backward(top_rows, agg_t, act_slope_t, top_grad, 2)
    second = gather(g_agg.astype(F32)[:ROWS], cb2, yb2, tab2)
    next(second)
    own_hidden = t_hidden.astype(F32)[:ROWS]
    ths[...] = own_hidden
    th_in = [send(ths, thr.at[0], dn_dev), send(ths, thr.at[1], up_dev)]
    pre_s = mm(s_close_rows, ws2) + mm(s_far_rows, wt2) + mb2
    s = sigmoid(pre_s)
    slope_s = s * (1.0 + pre_s * (1.0 - s))
    g_pre_t = mm(l_top[0:TILE, :], g_agg) * slope_t
    low_t = g_pre_t.astype(BF)
    dbm2 = jnp.sum(g_pre_t, axis=0, keepdims=True)
    a_half = a_cs.shape[1] - ROWS
    a_cs[1, 0:W, :] = tn(t_far_rows, low_t)
    a_cs[1, W : 2 * W, :] = tn(t_close_rows, low_t)
    a_cs[1, 2 * W : 3 * W, :] = dwn2_a
    a_cs[1, 3 * W : 4 * W, :] = dwn2_b
    g_nodes = g_nodes + nt_split(mm(t_scat, low_t), wt2)
    next(second)
    arrived(th_in)
    window = pad_rows(jnp.concatenate([thr[1], own_hidden, thr[0]], axis=0)).astype(BF)
    final = (c_hidden_f + mm(top_l, window)).astype(BF)[:nc]
    cfs[...] = final
    cf_in = [send(cfs, cfr, dn_dev)]
    next(second)
    arrived(cf_in)
    lift_rows = jnp.concatenate([final, cfr[...]], axis=0)
    next(second)
    lifted = mm(pool_l[...], lift_rows)
    out_ref[...] = ((hidden[...].astype(F32) + lifted) * alive).astype(BF)
    for _ in second:
        pass

    g_far = mm(o_top[TILE:, :], tab2[...].reshape(NP * ROWS, W))
    low_s = (g_far * slope_s).astype(BF)
    g_nodes = g_nodes + nt_split(mm(s_scat, low_s), ws2)
    g_own = g_nodes[:ROWS] / top_den
    gts[...] = g_own
    gt_in = [send(gts, gtr.at[0], dn_dev), send(gts, gtr.at[1], up_dev)]
    arrived(gt_in)
    window = pad_rows(jnp.concatenate([gtr[1], g_own, gtr[0]], axis=0))
    grad_coarse = pad_rows(grad_coarse0) + fold(mm(top_l, wide(window)))

    g_nodes, g_agg, dwn1_a, dwn1_b, dbn1 = node_backward(start_p, agg_c, act_slope_c, grad_coarse, 1)
    g_pre = mm(gcat[:, TILE:], g_agg) * slope_c
    dbm1 = jnp.sum(g_pre, axis=0, keepdims=True)
    sums = mm(gcat_t[...], g_pre.astype(BF))
    g_ext = nt_split(sums[:TILE], ws1)
    rgs[0] = g_ext[:rim]
    rgs[1] = g_ext[rim + nc : 2 * rim + nc]
    rg_in = [send(rgs.at[0], rgr.at[0], dn_dev), send(rgs.at[1], rgr.at[1], up_dev)]
    a_cs[0, 0:W, :] = fold(tn(cext, wide(sums[:TILE])))
    a_cs[0, W : 2 * W, :] = fold(tn(start_p, wide(sums[TILE:])))
    a_cs[0, 2 * W : 3 * W, :] = dwn1_a
    a_cs[0, 3 * W : 4 * W, :] = dwn1_b
    a_bias = jnp.concatenate([dbm1, dbn1, dbm2, dbn2, jnp.zeros((4, W), F32)], axis=0)
    a_cs[0, a_half:, :] = a_bias
    a_cs[1, a_half:, :] = a_bias
    g_start = (g_nodes + nt_split(sums[TILE:], wt1))[:nc] + g_ext[rim : rim + nc]

    scale = 1.0 / float(nf * NP) ** 0.5

    def reduce(cs, cr, xs, xr, zs, zr, yr, g, biases):
        copies = [send(cs.at[1 - c], cr, core_dev)]
        yield
        arrived(copies)
        part = cs[c] + cr[...]
        for sent, got, count, me, devs in ((xs, xr, X, gx, x_devs), (zs, zr, Z, z, z_devs)):
            n = sent.shape[1] - ROWS
            for j in range(count):
                sent[j, 0:n, :] = part[j * n : (j + 1) * n]
                sent[j, n:, :] = part[count * n :]
            copies = [
                send(sent.at[lax.rem(me + d + 1, count)], got.at[me], dev) for d, dev in enumerate(devs)
            ]
            got[me] = sent[me]
            yield
            arrived(copies)
            part = sum_slots(got, count)
        yr[y] = part
        copies = [send(yr.at[y], yr.at[y], dev) for dev in y_devs]
        yield
        arrived(copies)
        part = sum_slots(yr, Y) * scale
        n = g.shape[3]
        biases.append(part[n:])
        g[c, gx, z] = part[:n]
        copies = [send(g.at[c, gx, z], g.at[c, gx, z], dev) for dev in z_devs]
        yield
        arrived(copies)
        copies = [send(g.at[c, gx], g.at[c, gx], dev) for dev in x_devs]
        yield
        arrived(copies)
        copies = [send(g.at[c], g.at[c], core_dev)]
        yield
        arrived(copies)

    a_bias_out, f_bias_out = [], []
    reduce_a = reduce(a_cs, a_cr, a_xs, a_xr, a_zs, a_zr, a_yr, a_g, a_bias_out)
    next(reduce_a)
    arrived(rg_in)
    g_start = g_start + jnp.concatenate(
        [
            jnp.where(has_dn, rgr[1], 0.0),
            jnp.zeros((nc - 2 * rim, W), F32),
            jnp.where(has_up, rgr[0], 0.0),
        ],
        axis=0,
    )
    g_csum = g_start / den
    ugs[...] = g_csum.astype(BF)
    ug_in = [send(ugs, ugr, dn_dev)]
    next(reduce_a)
    arrived(ug_in)
    upper = jnp.where(has_up, ugr[...].astype(F32), 0.0)
    pool_grad = jnp.concatenate([g_csum, upper], axis=0)
    grad_fine = gout + fold(mm(pool_l[...], wide(pool_grad)))

    g_nodes, g_agg, dwn0_a, dwn0_b, dbn0 = node_backward(x_ref[...], aggf[...], act_slope[...], grad_fine, 0)
    aggf[...] = g_agg
    f_cs[1, 0:W, :] = dwn0_a
    f_cs[1, W : 2 * W, :] = dwn0_b

    def backward(k, total):
        at = pl.ds(pl.multiple_of(k * step, step), step)
        g_pre = mm(gat[at, ext_n:], aggf[...]) * slope[at, :]
        msgs[at, 0:W] = g_pre.astype(BF)
        return total + jnp.sum(g_pre, axis=0, keepdims=True)

    dbm0 = lax.fori_loop(0, ne // step, backward, jnp.zeros((1, W), F32))
    sums_h = mm(sca[nf:ext_n, :], msgs[:, 0:W])
    bgs[...] = nt_split(sums_h, ws0).astype(BF)
    bg_in = [
        send(bgs.at[0:halo_n], bgr.at[halo_n : 2 * halo_n], dn_dev),
        send(bgs.at[halo_n : 2 * halo_n], bgr.at[0:halo_n], up_dev),
    ]
    sums_s = mm(sca[0:nf, :], msgs[:, 0:W])
    sums_t = mm(sca[ext_n:, :], msgs[:, 0:W])
    f_cs[0, 0:W, :] = fold(tn(x_ref[...], wide(sums_s)) + tn(halo_f, wide(sums_h)))
    f_cs[0, W : 2 * W, :] = fold(tn(x_ref[...], wide(sums_t)))
    f_bias = jnp.concatenate([dbm0, dbn0, jnp.zeros((6, W), F32)], axis=0)
    f_half = f_cs.shape[1] - ROWS
    f_cs[0, f_half:, :] = f_bias
    f_cs[1, f_half:, :] = f_bias
    reduce_f = reduce(f_cs, f_cr, f_xs, f_xr, f_zs, f_zr, f_yr, f_g, f_bias_out)
    next(reduce_f)
    next(reduce_a)
    node_grad = g_nodes + nt_split(sums_s, ws0) + nt_split(sums_t, wt0)
    arrived(bg_in)
    live_back = (has_dn & (sub < halo_n)) | (has_up & (sub >= halo_n))
    back = jnp.where(live_back, bgr[...].astype(F32), 0.0).astype(BF)
    send_row = row(base_s)
    for g in range(nf // TILE):
        at = slice(g * TILE, (g + 1) * TILE)
        ngrad_ref[at, :] = node_grad[at] + mm(hot(sub + g * TILE == send_row), back)
    pending = [reduce_f, reduce_a]
    while pending:
        for item in list(pending):
            if next(item, 0) == 0:
                pending.remove(item)

    for copy in started:
        copy.wait_send()
    mwg_ref[0] = f_g[0].reshape(2 * W, W)
    nwg_ref[0] = f_g[1].reshape(2 * W, W)
    for level in (1, 2):
        both = a_g[level - 1].reshape(4 * W, W)
        mwg_ref[level] = both[: 2 * W]
        nwg_ref[level] = both[2 * W :]
    mbg_ref[0:1, :] = f_bias_out[0][0:1]
    nbg_ref[0:1, :] = f_bias_out[0][1:2]
    mbg_ref[1:2, :] = a_bias_out[0][0:1]
    nbg_ref[1:2, :] = a_bias_out[0][1:2]
    mbg_ref[2:3, :] = a_bias_out[0][2:3]
    nbg_ref[2:3, :] = a_bias_out[0][3:4]


def short_lists(
    split,
    fine_nodes, cotangent, msg_weights, msg_biases, node_weights, node_biases, node_count,
    fine_edges, fine_send, pool_map, coarse_edges, top_map, top_edges,
):
    Z, Y, C = split
    X = lax.axis_size("grp")
    NP = X * Z * Y * C
    nf = fine_nodes.shape[0]
    ne, nec, et = fine_edges.shape[2], coarse_edges.shape[2], top_edges.shape[1]
    nc = top_map.shape[1]
    nrow = et // TILE
    part = lax.axis_index(("grp", "dom"))
    rel = (top_map[0] - (part - 1) * ROWS) % (NP * ROWS)
    rel = jnp.concatenate([rel, jnp.full((TILE - nc,), -1, I32)])
    table = jnp.concatenate(
        [
            fine_edges.reshape(-1, TILE),
            coarse_edges.reshape(-1, TILE),
            fine_send.reshape(-1, TILE),
            pool_map.reshape(-1, TILE),
            rel.reshape(1, TILE),
        ]
    )
    table = jnp.pad(table, ((0, -table.shape[0] % 8), (0, 0)))
    tops = jnp.pad(
        top_edges.reshape(2, nrow, TILE), ((0, 0), (0, TILE - nrow), (0, 0)), constant_values=-1
    ).reshape(2 * TILE, TILE)
    vm = lambda *shape: pltpu.VMEM(shape, F32)
    vb = lambda *shape: pltpu.VMEM(shape, BF)
    ext_n = nf + 128
    gathers = [vm(16, W), vb(Y, 16, W), vb(2, X * Z, Y * ROWS, W)]

    def reduce_bufs(total):
        r = total // 2 // X // Z
        return [
            vm(2, total // 2 + ROWS, W),
            vm(total // 2 + ROWS, W),
            vm(X, r * Z + ROWS, W),
            vm(X, r * Z + ROWS, W),
            vm(Z, r + ROWS, W),
            vm(Z, r + ROWS, W),
            vm(Y, r + ROWS, W),
            vm(2, X, Z, r, W),
        ]

    scratch = [
        vb(ne, ext_n + nf), vb(ext_n + nf, ne), vb(ext_n + nf, 2 * W), vm(ne, W), vb(ne, 2 * W),
        vm(nf, W), vb(nf, W), vb(nf, W), vb(TILE, nf), vb(nf, TILE),
        vb(nec, 2 * TILE), vb(2 * TILE, nec), vb(2 * TILE, NP * ROWS), vb(2 * TILE, TILE),
        vm(TILE, TILE), vm(TILE, TILE),
        vb(128, W), vb(128, W), vm(2 * nc, W), vm(2 * nc, W), vm(2, 16, W), vm(2, 16, W),
        vm(nc, W), vm(nc, W), vm(2, 8, W), vm(2, 8, W), vm(2, 8, W), vm(2, 8, W),
        *gathers, *gathers,
        vm(8, W), vm(2, 8, W), vb(nc, W), vb(nc, W), vm(8, W), vm(2, 8, W),
        vm(2, 8, W), vm(2, 8, W), vb(nc, W), vb(nc, W), vb(128, W), vb(128, W),
        *reduce_bufs(4 * W), *reduce_bufs(8 * W),
    ]
    copies = 20 + 2 * (2 + (X - 1) + (Z - 1) + (Y - 1)) + 2 * (2 + 2 * (X - 1) + 2 * (Z - 1) + (Y - 1))
    scratch += [pltpu.SemaphoreType.DMA((copies + 4,)), pltpu.SemaphoreType.DMA((copies + 4,))]
    in_vmem = pl.BlockSpec(memory_space=pltpu.VMEM)
    sizes = (X, Z, Y, C, nf, ne, nc, nec, nrow)
    grads = jax.ShapeDtypeStruct(msg_weights.shape, F32)
    biases = jax.ShapeDtypeStruct(msg_biases.shape, F32)
    outs = pl.pallas_call(
        functools.partial(step_kernel, sizes),
        out_shape=[
            jax.ShapeDtypeStruct((nf, W), BF),
            jax.ShapeDtypeStruct((nf, W), F32),
            grads, biases, grads, biases,
        ],
        in_specs=[in_vmem] * 6 + [pl.BlockSpec(memory_space=pltpu.SMEM)] + [in_vmem] * 2,
        out_specs=[in_vmem] * 6,
        scratch_shapes=scratch,
        compiler_params=pltpu.CompilerParams(
            collective_id=0, has_side_effects=True, vmem_limit_bytes=48 * 1024 * 1024
        ),
        name="step",
    )(
        fine_nodes, cotangent, msg_weights, msg_biases, node_weights, node_biases, node_count,
        table, tops,
    )
    return tuple(outs)


def per_device(split, *args):
    owner = args[-1] // ROWS
    digits = jnp.arange(16)[None, :, None]
    high = (owner[:, None, :] // 16 == digits).astype(BF)
    low = (owner[:, None, :] % 16 == digits).astype(BF)
    counts = jnp.einsum("khe,kle->khl", high, low, preferred_element_type=F32)
    return lax.cond(
        jnp.max(counts) <= CAP, functools.partial(short_lists, split), any_lists, *args
    )


def solution(mesh):
    return jax.shard_map(
        functools.partial(per_device, DOM_SPLIT),
        mesh=mesh,
        in_specs=(
            P(("grp", "dom"), None),
            P(("grp", "dom"), None),
            P(),
            P(),
            P(),
            P(),
            P(("grp", "dom")),
            P(("grp", "dom"), None, None),
            P(("grp", "dom"), None, None),
            P(("grp", "dom"), None),
            P(("grp", "dom"), None, None),
            P(("grp", "dom"), None),
            P(),
        ),
        out_specs=(P(("grp", "dom"), None), P(("grp", "dom"), None), P(), P(), P(), P()),
        check_vma=False,
    )
```

```python
import functools

import jax
import jax.numpy as jnp
from jax import lax
from jax.experimental import pallas as pl
from jax.experimental.pallas import tpu as pltpu
from jax.sharding import PartitionSpec as P

BF, F32, I32 = jnp.bfloat16, jnp.float32, jnp.int32
MESH = pl.DeviceIdType.MESH
W = 128
TILE = 128
CAP = 128
DOM_SPLIT = (8, 4, 2)
ROWS = 8


def mm(a, b):
    return jnp.dot(a, b, preferred_element_type=F32)


def nt(a, b):
    return lax.dot_general(a, b, (((1,), (1,)), ((), ())), preferred_element_type=F32)


def tn(a, b):
    return lax.dot_general(a, b, (((0,), (0,)), ((), ())), preferred_element_type=F32)


def wide(v):
    high = v.astype(BF)
    return jnp.concatenate([high, (v - high.astype(F32)).astype(BF)], axis=1)


def fold(v):
    return v[:, :W] + v[:, W:]


def nt_split(v, weight):
    high = v.astype(BF)
    return nt(high, weight) + nt((v - high.astype(F32)).astype(BF), weight)


def iota(shape, dim):
    return lax.broadcasted_iota(I32, shape, dim)


def hot(mask):
    return jnp.where(mask, 1.0, 0.0).astype(BF)


def down_lanes(row):
    return jnp.transpose(jnp.broadcast_to(row, (TILE, TILE)))


def sigmoid(v):
    return 0.5 * jnp.tanh(0.5 * v) + 0.5


def pad_rows(v, total=TILE):
    return jnp.concatenate([v, jnp.zeros((total - v.shape[0], v.shape[1]), v.dtype)], axis=0)


def sum_slots(ref, count):
    total = ref[0]
    for slot in range(1, count):
        total = total + ref[slot]
    return total


def step_kernel(
    sizes, packed,
    x_in, cot_in, mw_in, mb_in, nw_in, nb_in, cnt_ref, fe_in, fs_in, pm_in, ce_in, tm_in, te_in,
    out_to, ngrad_to, par_to,
    x_ref, cot_ref, mw_ref, mb_ref, nw_ref, nb_ref, fe_ref, fs_ref, pm_ref, ce_ref, tm_ref, te_ref,
    out_ref, ngrad_ref, par_ref, lsem,
    sums_r, kept, gat, sca, hl, slope, msgs, act_slope, hidden, aggf, pool_t, pool_l,
    gcat, gcat_t, o_top, l_top, sc_top, te_s, pos_s, key_s,
    sendbuf, halo, e0s, e0r, e0d, e0dr, e0u, e0ur, e1s, e1r, pss, psr, psd, psdr, psu, psur, tss, tsr,
    cb1, tab1, cb2, tab2, ths, thr, cfs, cfr, gts, gtr, rgs, rgr, rus, rur, rdr, bgs, bgr,
    f_cs, f_cr, f_xs, f_xr, f_zr, f_g,
    a_cs, a_cr, a_xs, a_xr, a_zr, a_g,
    ssem, rsem,
):
    X, Z, Y, C, nf, ne, nc, nec, nrow = sizes
    DOM = Z * Y * C
    NP = X * DOM
    halo_n = 64
    ext_n = nf + 2 * halo_n
    rim = nc // 8
    gx = lax.axis_index("grp")
    dm = lax.axis_index("dom")
    p = gx * DOM + dm
    z = lax.div(dm, Y * C)
    y = lax.rem(lax.div(dm, C), Y)
    c = lax.rem(dm, C)
    xz = gx * Z + z
    up = lax.rem(p + 1, NP)
    dn = lax.rem(p + NP - 1, NP)
    has_dn = p > 0
    has_up = p < NP - 1
    up2 = lax.rem(p + 2, NP)
    dn2 = lax.rem(p + NP - 2, NP)
    has_dn2 = p > 1
    has_up2 = p < NP - 2
    XY = X * Y
    ZC = Z * C
    xy = gx * Y + y
    zc = z * C + c

    def spot_of(q):
        return (lax.div(q, DOM), lax.rem(q, DOM))

    def plane(q):
        return (lax.div(q, Y), z * (Y * C) + lax.rem(q, Y) * C + c)

    def column(q):
        return (gx, lax.div(q, C) * (Y * C) + y * C + lax.rem(q, C))

    up_dev, dn_dev, up2_dev, dn2_dev = spot_of(up), spot_of(dn), spot_of(up2), spot_of(dn2)
    core_dev = (gx, dm + 1 - 2 * c)
    plane_devs = [plane(lax.rem(xy + d, XY)) for d in range(1, XY)]
    column_devs = [column(lax.rem(zc + d, ZC)) for d in range(1, ZC)]
    z_devs = [column(lax.rem(zc + d * C, ZC)) for d in range(1, Z)]

    loads = {}
    for spot, (name, src, dst) in enumerate(
        (
            ("fs", fs_in, fs_ref), ("x", x_in, x_ref), ("pm", pm_in, pm_ref), ("cot", cot_in, cot_ref),
            ("tm", tm_in, tm_ref), ("fe", fe_in, fe_ref), ("mw", mw_in, mw_ref), ("mb", mb_in, mb_ref),
            ("ce", ce_in, ce_ref), ("te", te_in, te_ref), ("nw", nw_in, nw_ref), ("nb", nb_in, nb_ref),
        )
    ):
        loads[name] = pltpu.make_async_copy(src, dst, lsem.at[spot])
        loads[name].start()
    barrier = pltpu.get_barrier_semaphore()
    partners = [up_dev, dn_dev, up2_dev, dn2_dev] + plane_devs + column_devs
    for dev in partners:
        pl.semaphore_signal(barrier, inc=1, device_id=dev, device_id_type=MESH)

    started = []

    def send(src, dst, dev):
        spot = len(started)
        copy = pltpu.make_async_remote_copy(
            src_ref=src, dst_ref=dst, send_sem=ssem.at[spot], recv_sem=rsem.at[spot],
            device_id=dev, device_id_type=MESH,
        )
        copy.start()
        started.append(copy)
        return copy

    def arrived(copies):
        for copy in copies:
            copy.wait_recv()

    ntile = ne // TILE
    ctile = nec // TILE
    lane = iota((TILE, TILE), 1)
    sub = iota((TILE, TILE), 0)
    ones = jnp.ones((TILE, TILE), BF)

    loads["fs"].wait()
    loads["x"].wait()
    send_row = jnp.concatenate([fs_ref[0, 0:1, :], fs_ref[0, 1:2, :]], axis=1)
    send_lanes = down_lanes(send_row)
    picks = jnp.concatenate([hot(send_lanes == lane + g * TILE) for g in range(nf // TILE)], axis=1)
    sendbuf[...] = mm(picks, x_ref[...]).astype(BF)
    pl.semaphore_wait(barrier, len(partners))
    halo_in = [
        send(sendbuf.at[halo_n : 2 * halo_n], halo.at[0:halo_n], up_dev),
        send(sendbuf.at[0:halo_n], halo.at[halo_n : 2 * halo_n], dn_dev),
    ]

    loads["pm"].wait()
    loads["cot"].wait()
    loads["tm"].wait()
    live = cnt_ref[0]
    alive = jnp.where(iota((nf, W), 0) < live, 1.0, 0.0)
    for g in range(nf // TILE):
        keys = pm_ref[0:1, g * TILE : (g + 1) * TILE]
        pool_t[:, g * TILE : (g + 1) * TILE] = hot((sub == keys) & (lane + g * TILE < live))
        pool_l[g * TILE : (g + 1) * TILE, :] = hot((down_lanes(keys) == lane) & (sub + g * TILE < live))
    gout = cot_ref[...] * alive
    counts = mm(pool_t[...], jnp.ones((nf, W), BF))
    lift = fold(mm(pool_t[...], wide(gout)))
    e0s[0:nc, :] = lift[nc:]
    e0s[nc : 2 * nc + rim, :] = jnp.concatenate([counts[nc:], counts[nc - rim : nc]], axis=0)
    e0d[...] = counts[:nc]
    e0u[...] = counts[2 * nc - rim :]
    e0_in = [send(e0s, e0r, up_dev), send(e0d, e0dr, dn_dev), send(e0u, e0ur, up2_dev)]
    rel = lax.rem(tm_ref[...] - (p - 1) * ROWS + NP * ROWS, NP * ROWS)
    rel = jnp.concatenate([rel, jnp.full((1, TILE - nc), -1, I32)], axis=1)
    top_t = hot(sub == rel)
    top_l = hot(down_lanes(rel) == lane)
    top_counts = mm(top_t, ones)

    loads["fe"].wait()

    def build(k, carry):
        at = pl.ds(pl.multiple_of(k * TILE, TILE), TILE)
        src, tgt = fe_ref[0, 0:1, at], fe_ref[0, 1:2, at]
        src_lanes, tgt_lanes = down_lanes(src), down_lanes(tgt)
        for g in range(ext_n // TILE):
            gat[at, g * TILE : (g + 1) * TILE] = hot(src_lanes == lane + g * TILE)
            sca[g * TILE : (g + 1) * TILE, at] = hot(sub + g * TILE == src)
        for g in range(nf // TILE):
            gat[at, ext_n + g * TILE : ext_n + (g + 1) * TILE] = hot(tgt_lanes == lane + g * TILE)
            sca[ext_n + g * TILE : ext_n + (g + 1) * TILE, at] = hot(sub + g * TILE == tgt)
        return carry

    lax.fori_loop(0, ntile, build, 0)
    loads["mw"].wait()
    loads["mb"].wait()
    ws0, wt0 = mw_ref[0, :W, :], mw_ref[0, W:, :]
    hl[0:nf, :] = wide(mm(x_ref[...], ws0))
    hl[ext_n : ext_n + nf, :] = wide(mm(x_ref[...], wt0) + mb_ref[0:1, :])

    loads["ce"].wait()
    for k in range(ctile):
        src = ce_ref[0, 0:1, k * TILE : (k + 1) * TILE]
        tgt = ce_ref[0, 1:2, k * TILE : (k + 1) * TILE]
        gcat[k * TILE : (k + 1) * TILE, 0:TILE] = hot(down_lanes(src) == lane)
        gcat[k * TILE : (k + 1) * TILE, TILE:] = hot(down_lanes(tgt) == lane)
        gcat_t[0:TILE, k * TILE : (k + 1) * TILE] = hot(sub == src)
        gcat_t[TILE:, k * TILE : (k + 1) * TILE] = hot(sub == tgt)

    first = p * ROWS
    loads["te"].wait()
    loads["nw"].wait()
    loads["nb"].wait()
    te_s[...] = jnp.full(te_s.shape, -1, I32)

    def lay(r, carry):
        at = pl.ds(pl.multiple_of(r * TILE, TILE), TILE)
        te_s[pl.ds(r, 1), :] = te_ref[0:1, at]
        te_s[pl.ds(TILE + r, 1), :] = te_ref[1:2, at]
        return carry

    lax.fori_loop(0, nrow, lay, 0)

    def owned(values):
        return (values >= first) & (values < first + ROWS)

    def keys_of(src, tgt):
        return (src * (NP * ROWS) + tgt + 1).astype(F32)

    def ends(key):
        code = key.astype(I32) - 1
        empty = code < 0
        return (
            jnp.where(empty, -1, lax.div(code, NP * ROWS)),
            jnp.where(empty, -1, lax.rem(code, NP * ROWS)),
        )

    half = ZC * ROWS // 2

    def place(node):
        part = lax.div(node, ROWS)
        core = lax.rem(part, C)
        py = lax.rem(lax.div(part, C), Y)
        pz = lax.rem(lax.div(part, C * Y), Z)
        px = lax.div(part, C * Y * Z)
        inner = (pz * C + core) * ROWS + lax.rem(node, ROWS)
        spot = lax.div(inner, half) * (XY * half) + (px * Y + py) * half + lax.rem(inner, half)
        return jnp.where(node < 0, -1, spot)

    near = jnp.where(lane < ROWS, lane + first, -2)
    near_t = jnp.where(sub < ROWS, sub + first, -2)

    def fill(t_lanes, s_lanes):
        (t_src, t_tgt), (s_src, s_tgt) = ends(t_lanes), ends(s_lanes)
        t_far, s_far = place(t_src), place(s_tgt)
        for g in range(NP * ROWS // TILE):
            o_top[0:TILE, g * TILE : (g + 1) * TILE] = hot(t_far == lane + g * TILE)
            o_top[TILE:, g * TILE : (g + 1) * TILE] = hot(s_far == lane + g * TILE)
        l_top[0:TILE, :] = hot(t_tgt == near)
        l_top[TILE:, :] = hot(s_src == near)
        sc_top[0:TILE, :] = hot(ends(jnp.transpose(t_lanes))[1] == near_t)
        sc_top[TILE:, :] = hot(ends(jnp.transpose(s_lanes))[0] == near_t)

    def fill_row(r):
        src, tgt = te_s[pl.ds(r, 1), :], te_s[pl.ds(TILE + r, 1), :]
        key = keys_of(src, tgt)
        fill(
            down_lanes(jnp.where(owned(tgt), key, 0.0)), down_lanes(jnp.where(owned(src), key, 0.0))
        )

    if packed:
        upper_ones = hot(sub <= lane)
        lower_ones = hot(lane < sub)
        sub_f = sub.astype(F32)
        key_s[...] = keys_of(te_s[0:TILE, :], te_s[TILE:, :])
        lists = []
        for values in (te_s[TILE:, :], te_s[0:TILE, :]):
            mine = owned(values)
            flags = hot(mine)
            offset = mm(lower_ones, mm(flags, ones).astype(BF))
            pos_s[...] = jnp.where(mine, mm(flags, upper_ones) + offset - 1.0, -1.0)

            def pick(r, acc):
                at = pl.ds(pl.multiple_of(r * 8, 8), 8)
                places, keys8 = pos_s[at, :], key_s[at, :]
                for i in range(8):
                    acc = acc + jnp.where(places[i : i + 1, :] == sub_f, keys8[i : i + 1, :], 0.0)
                return acc

            acc = lax.fori_loop(0, -(-nrow // 8), pick, jnp.zeros((TILE, TILE), F32))
            lists.append(jnp.broadcast_to(jnp.sum(acc, axis=1, keepdims=True), (TILE, TILE)))
        fill(*lists)

    arrived(e0_in)
    lower = jnp.where(has_dn, e0r[0 : 2 * nc, :], 0.0)
    grad_coarse0 = lift[:nc] + lower[:nc]
    den = jnp.maximum(counts[:nc] + lower[nc:], 1.0)
    den_up = jnp.maximum(e0dr[...] + counts[nc:], 1.0)
    den_dn = jnp.maximum(e0r[2 * nc :, :] + jnp.where(has_dn2, e0ur[...], 0.0), 1.0)
    top_g = fold(mm(top_t, pad_rows(wide(grad_coarse0))))
    e1s[0, 0:ROWS, :] = top_counts[0:ROWS]
    e1s[0, ROWS:, :] = top_g[0:ROWS]
    e1s[1, 0:ROWS, :] = top_counts[2 * ROWS : 3 * ROWS]
    e1s[1, ROWS:, :] = top_g[2 * ROWS : 3 * ROWS]
    e1_in = [send(e1s.at[0], e1r.at[0], dn_dev), send(e1s.at[1], e1r.at[1], up_dev)]

    arrived(halo_in)
    halo_rows = sub
    live_halo = (has_dn & (halo_rows < halo_n)) | (has_up & (halo_rows >= halo_n))
    halo_f = jnp.where(live_halo, halo[...].astype(F32), 0.0).astype(BF)
    hl[nf:ext_n, :] = wide(mm(halo_f, ws0))
    step = 4 * TILE

    def forward(k, carry):
        at = pl.ds(pl.multiple_of(k * step, step), step)
        pre = fold(mm(gat[at, :], hl[...]))
        s = sigmoid(pre)
        slope[at, :] = s * (1.0 + pre * (1.0 - s))
        msgs[at, :] = wide(pre * s)
        return carry

    lax.fori_loop(0, ne // step, forward, 0)

    def node_forward(rows, agg, level):
        act = mm(rows, nw_ref[level, :W, :]) + mm(agg, nw_ref[level, W:, :]) + nb_ref[level : level + 1, :]
        s = sigmoid(act)
        return (rows.astype(F32) + act * s).astype(BF), s * (1.0 + act * (1.0 - s))

    def node_backward(rows, agg, act_slopes, grad, level):
        g_act = grad * act_slopes
        low = g_act.astype(BF)
        pair = nt(low, nw_ref[level])
        return (
            grad + pair[:, :W],
            pair[:, W:].astype(BF),
            tn(rows, low),
            tn(agg, low),
            jnp.sum(g_act, axis=0, keepdims=True),
        )

    for k in range(nf // step):
        at = slice(k * step, (k + 1) * step)
        agg = fold(mm(sca[ext_n + k * step : ext_n + (k + 1) * step, :], msgs[...])).astype(BF)
        new, act_s = node_forward(x_ref[at, :], agg, 0)
        aggf[at, :] = agg
        hidden[at, :] = new
        act_slope[at, :] = act_s

    pooled = mm(pool_t[...], hidden[...])
    pss[...] = pooled[nc - rim :]
    psd[...] = pooled[:rim]
    psu[...] = pooled[2 * nc - rim :]
    ps_in = [send(pss, psr, up_dev), send(psd, psdr, dn_dev), send(psu, psur, up2_dev)]
    arrived(e1_in)
    own_win = slice(ROWS, 2 * ROWS)
    top_den = jnp.maximum(top_counts[own_win] + e1r[0, 0:ROWS, :] + e1r[1, 0:ROWS, :], 1.0)
    top_grad = pad_rows(top_g[own_win] + e1r[0, ROWS:, :] + e1r[1, ROWS:, :])
    arrived(ps_in)
    start_f = ((pooled[:nc] + jnp.where(has_dn, psr[rim:, :], 0.0)) / den).astype(BF).astype(F32)
    left = (psr[0:rim, :] + jnp.where(has_dn2, psur[...], 0.0)) / den_dn
    right = (psdr[...] + pooled[nc : nc + rim]) / den_up[:rim]
    start_p = pad_rows(start_f).astype(BF)
    ws1, wt1 = mw_ref[1, :W, :], mw_ref[1, W:, :]
    near_part = wide(mm(start_p, wt1) + mb_ref[1:2, :])
    cext = pad_rows(
        jnp.concatenate(
            [jnp.where(has_dn, left, 0.0), start_f, jnp.where(has_up, right, 0.0)], axis=0
        )
    ).astype(BF)
    pre = fold(mm(gcat[...], jnp.concatenate([wide(mm(cext, ws1)), near_part], axis=0)))
    s = sigmoid(pre)
    slope_c = s * (1.0 + pre * (1.0 - s))
    agg_c = fold(mm(gcat_t[TILE:, :], wide(pre * s))).astype(BF)
    c_hidden, act_slope_c = node_forward(start_p, agg_c, 1)
    keep = sub < nc
    c_hidden_f = jnp.where(keep, c_hidden.astype(F32), 0.0)
    top_part = mm(top_t, c_hidden_f.astype(BF))
    tss[0] = top_part[0:ROWS]
    tss[1] = top_part[2 * ROWS : 3 * ROWS]
    ts_in = [send(tss.at[0], tsr.at[0], dn_dev), send(tss.at[1], tsr.at[1], up_dev)]
    arrived(ts_in)
    top_start = ((top_part[own_win] + tsr[0] + tsr[1]) / top_den).astype(BF)

    def gather(own, cb, tab):
        cb[zc] = own
        copies = [send(cb.at[zc], cb.at[zc], dev) for dev in column_devs]
        yield
        arrived(copies)
        tab[c, xy] = cb[pl.ds(c * (ZC // 2), ZC // 2)].reshape(half, W).astype(BF)
        copies = [send(tab.at[c, xy], tab.at[c, xy], dev) for dev in plane_devs]
        yield
        arrived(copies)
        copies = [send(tab.at[c], tab.at[c], core_dev)]
        yield
        arrived(copies)

    for _ in gather(top_start.astype(F32), cb1, tab1):
        pass

    ws2, wt2, mb2 = mw_ref[2, :W, :], mw_ref[2, W:, :], mb_ref[2:3, :]
    top_rows = pad_rows(top_start.astype(F32)).astype(BF)
    kept[:, 0:W] = top_rows

    def t_edges():
        far = mm(o_top[0:TILE, :], tab1[...].reshape(NP * ROWS, W)).astype(BF)
        close = mm(l_top[0:TILE, :], kept[:, 0:W]).astype(BF)
        pre_t = mm(far, ws2) + mm(close, wt2) + mb2
        s = sigmoid(pre_t)
        return far, close, pre_t * s, s * (1.0 + pre_t * (1.0 - s))

    def t_sums(message):
        return fold(mm(sc_top[0:TILE, :], wide(message)))

    def t_back(far, close, slope_t):
        g_pre_t = mm(l_top[0:TILE, :], kept[:, W:]) * slope_t
        low_t = g_pre_t.astype(BF)
        return (
            tn(far, low_t),
            tn(close, low_t),
            mm(sc_top[0:TILE, :], low_t),
            jnp.sum(g_pre_t, axis=0, keepdims=True),
        )

    def s_slopes():
        far = mm(o_top[TILE:, :], tab1[...].reshape(NP * ROWS, W)).astype(BF)
        close = mm(l_top[TILE:, :], kept[:, 0:W]).astype(BF)
        pre_s = mm(close, ws2) + mm(far, wt2) + mb2
        s = sigmoid(pre_s)
        return s * (1.0 + pre_s * (1.0 - s))

    def s_back(slope_s):
        g_far = mm(o_top[TILE:, :], tab2[...].reshape(NP * ROWS, W))
        return mm(sc_top[TILE:, :], (g_far * slope_s).astype(BF))

    def over_rows(work):
        sums_r[...] = jnp.zeros(sums_r.shape, F32)

        def one(r, carry):
            fill_row(r)
            for spot, term in enumerate(work()):
                sums_r[spot, 0 : term.shape[0], :] += term
            return carry

        lax.fori_loop(0, nrow, one, 0)

    def t_back_row():
        far = mm(o_top[0:TILE, :], tab1[...].reshape(NP * ROWS, W)).astype(BF)
        both = mm(l_top[0:TILE, :], kept[...])
        close = both[:, 0:W].astype(BF)
        pre_t = mm(far, ws2) + mm(close, wt2) + mb2
        s = sigmoid(pre_t)
        g_pre_t = both[:, W:] * (s * (1.0 + pre_t * (1.0 - s)))
        low_t = g_pre_t.astype(BF)
        return (
            tn(far, low_t),
            tn(close, low_t),
            mm(sc_top[0:TILE, :], low_t),
            jnp.sum(g_pre_t, axis=0, keepdims=True),
        )

    if packed:
        t_far_rows, t_close_rows, message, slope_t = t_edges()
        agg_t = t_sums(message).astype(BF)
    else:
        over_rows(lambda: (t_sums(t_edges()[2]),))
        agg_t = sums_r[0].astype(BF)
    t_hidden, act_slope_t = node_forward(top_rows, agg_t, 2)
    g_nodes, g_agg, dwn2_a, dwn2_b, dbn2 = node_backward(top_rows, agg_t, act_slope_t, top_grad, 2)
    kept[:, W:] = g_agg
    key_s[...] = g_nodes
    a_cs[1, 2 * W : 3 * W, :] = dwn2_a
    a_cs[1, 3 * W : 4 * W, :] = dwn2_b
    second = gather(g_agg.astype(F32)[:ROWS], cb2, tab2)
    next(second)
    own_hidden = t_hidden.astype(F32)[:ROWS]
    ths[...] = own_hidden
    th_in = [send(ths, thr.at[0], dn_dev), send(ths, thr.at[1], up_dev)]
    if packed:
        slope_s = s_slopes()
        backs = t_back(t_far_rows, t_close_rows, slope_t)
    else:
        over_rows(t_back_row)
        backs = sums_r[0], sums_r[1], sums_r[2], sums_r[3, 0:1, :]
    dwm2_a, dwm2_b, sums_t, dbm2 = backs
    a_half = a_cs.shape[1] - ROWS
    a_cs[1, 0:W, :] = dwm2_a
    a_cs[1, W : 2 * W, :] = dwm2_b
    g_nodes = key_s[...] + nt_split(sums_t, wt2)
    next(second)
    arrived(th_in)
    window = pad_rows(jnp.concatenate([thr[1], own_hidden, thr[0]], axis=0)).astype(BF)
    final = (c_hidden_f + mm(top_l, window)).astype(BF)[:nc]
    cfs[...] = final
    cf_in = [send(cfs, cfr, dn_dev)]
    arrived(cf_in)
    lift_rows = jnp.concatenate([final, cfr[...]], axis=0)
    lifted = mm(pool_l[...], lift_rows)
    out_ref[...] = ((hidden[...].astype(F32) + lifted) * alive).astype(BF)
    stores = [pltpu.make_async_copy(out_ref, out_to, lsem.at[12])]
    stores[0].start()
    for _ in second:
        pass

    if packed:
        sums_s = s_back(slope_s)
    else:
        over_rows(lambda: (s_back(s_slopes()),))
        sums_s = sums_r[0]
    g_nodes = g_nodes + nt_split(sums_s, ws2)
    g_own = g_nodes[:ROWS] / top_den
    gts[...] = g_own
    gt_in = [send(gts, gtr.at[0], dn_dev), send(gts, gtr.at[1], up_dev)]
    arrived(gt_in)
    window = pad_rows(jnp.concatenate([gtr[1], g_own, gtr[0]], axis=0))
    grad_coarse = pad_rows(grad_coarse0) + fold(mm(top_l, wide(window)))

    g_nodes, g_agg, dwn1_a, dwn1_b, dbn1 = node_backward(start_p, agg_c, act_slope_c, grad_coarse, 1)
    g_pre = mm(gcat[:, TILE:], g_agg) * slope_c
    dbm1 = jnp.sum(g_pre, axis=0, keepdims=True)
    sums = mm(gcat_t[...], g_pre.astype(BF))
    g_ext = nt_split(sums[:TILE], ws1)
    g_start = (g_nodes + nt_split(sums[TILE:], wt1))[:nc] + g_ext[rim : rim + nc]
    rgs[0:nc, :] = g_start
    rgs[nc:, :] = g_ext[:rim]
    rus[...] = g_ext[rim + nc : 2 * rim + nc]
    rg_in = [
        send(rgs, rgr, dn_dev),
        send(rus, rur, up_dev),
        send(rgs.at[nc : nc + rim], rdr, dn2_dev),
    ]
    a_cs[0, 0:W, :] = fold(tn(cext, wide(sums[:TILE])))
    a_cs[0, W : 2 * W, :] = fold(tn(start_p, wide(sums[TILE:])))
    a_cs[0, 2 * W : 3 * W, :] = dwn1_a
    a_cs[0, 3 * W : 4 * W, :] = dwn1_b
    a_bias = jnp.concatenate([dbm1, dbn1, dbm2, dbn2, jnp.zeros((4, W), F32)], axis=0)
    a_cs[0, a_half:, :] = a_bias
    a_cs[1, a_half:, :] = a_bias

    scale = 1.0 / float(nf * NP) ** 0.5

    def reduce(cs, cr, xs, xr, zr, g, biases):
        copies = [send(cs.at[1 - c], cr, core_dev)]
        yield
        arrived(copies)
        part = cs[c] + cr[...]
        n = g.shape[2]
        for j in range(XY):
            xs[j, 0:n, :] = part[j * n : (j + 1) * n]
            xs[j, n:, :] = part[XY * n :]
        copies = [
            send(xs.at[lax.rem(xy + d + 1, XY)], xr.at[xy], dev) for d, dev in enumerate(plane_devs)
        ]
        xr[xy] = xs[xy]
        yield
        arrived(copies)
        zr[z] = sum_slots(xr, XY)
        copies = [send(zr.at[z], zr.at[z], dev) for dev in z_devs]
        yield
        arrived(copies)
        part = sum_slots(zr, Z) * scale
        biases.append(part[n:])
        g[c, xy] = part[:n]
        copies = [send(g.at[c, xy], g.at[c, xy], dev) for dev in plane_devs]
        yield
        arrived(copies)
        copies = [send(g.at[c], g.at[c], core_dev)]
        yield
        arrived(copies)

    a_bias_out, f_bias_out = [], []
    reduce_a = reduce(a_cs, a_cr, a_xs, a_xr, a_zr, a_g, a_bias_out)
    next(reduce_a)
    arrived(rg_in)
    middle = jnp.zeros((nc - 2 * rim, W), F32)
    g_csum = (
        g_start
        + jnp.concatenate(
            [jnp.where(has_dn, rur[...], 0.0), middle, jnp.where(has_up, rgr[nc:, :], 0.0)], axis=0
        )
    ) / den
    upper = (
        rgr[0:nc, :] + jnp.concatenate([rus[...], middle, jnp.where(has_up2, rdr[...], 0.0)], axis=0)
    ) / den_up
    pool_grad = jnp.concatenate([g_csum, jnp.where(has_up, upper, 0.0)], axis=0)
    next(reduce_a)
    grad_fine = gout + fold(mm(pool_l[...], wide(pool_grad)))

    g_nodes, g_agg, dwn0_a, dwn0_b, dbn0 = node_backward(x_ref[...], aggf[...], act_slope[...], grad_fine, 0)
    aggf[...] = g_agg
    f_cs[1, 0:W, :] = dwn0_a
    f_cs[1, W : 2 * W, :] = dwn0_b

    def backward(k, total):
        at = pl.ds(pl.multiple_of(k * step, step), step)
        g_pre = mm(gat[at, ext_n:], aggf[...]) * slope[at, :]
        msgs[at, 0:W] = g_pre.astype(BF)
        return total + jnp.sum(g_pre, axis=0, keepdims=True)

    dbm0 = lax.fori_loop(0, ne // step, backward, jnp.zeros((1, W), F32))
    sums_h = mm(sca[nf:ext_n, :], msgs[:, 0:W])
    bgs[...] = nt_split(sums_h, ws0).astype(BF)
    bg_in = [
        send(bgs.at[0:halo_n], bgr.at[halo_n : 2 * halo_n], dn_dev),
        send(bgs.at[halo_n : 2 * halo_n], bgr.at[0:halo_n], up_dev),
    ]
    sums_s = mm(sca[0:nf, :], msgs[:, 0:W])
    sums_t = mm(sca[ext_n:, :], msgs[:, 0:W])
    f_cs[0, 0:W, :] = fold(tn(x_ref[...], wide(sums_s)) + tn(halo_f, wide(sums_h)))
    f_cs[0, W : 2 * W, :] = fold(tn(x_ref[...], wide(sums_t)))
    f_bias = jnp.concatenate([dbm0, dbn0, jnp.zeros((6, W), F32)], axis=0)
    f_half = f_cs.shape[1] - ROWS
    f_cs[0, f_half:, :] = f_bias
    f_cs[1, f_half:, :] = f_bias
    reduce_f = reduce(f_cs, f_cr, f_xs, f_xr, f_zr, f_g, f_bias_out)
    next(reduce_f)
    next(reduce_a)
    node_grad = g_nodes + nt_split(sums_s, ws0) + nt_split(sums_t, wt0)
    arrived(bg_in)
    live_back = (has_dn & (sub < halo_n)) | (has_up & (sub >= halo_n))
    back = jnp.where(live_back, bgr[...].astype(F32), 0.0).astype(BF)
    for g in range(nf // TILE):
        at = slice(g * TILE, (g + 1) * TILE)
        ngrad_ref[at, :] = node_grad[at] + mm(hot(sub + g * TILE == send_row), back)
    stores.append(pltpu.make_async_copy(ngrad_ref, ngrad_to, lsem.at[13]))
    stores[1].start()
    pending = [reduce_f, reduce_a]
    while pending:
        for item in list(pending):
            if next(item, 0) == 0:
                pending.remove(item)

    for copy in started:
        copy.wait_send()
    par_ref[0 : 4 * W, :] = f_g[...].reshape(4 * W, W)
    par_ref[4 * W : 12 * W, :] = a_g[...].reshape(8 * W, W)
    par_ref[12 * W : 12 * W + 8, :] = f_bias_out[0]
    par_ref[12 * W + 8 :, :] = a_bias_out[0]
    stores.append(pltpu.make_async_copy(par_ref, par_to, lsem.at[14]))
    stores[2].start()
    for copy in stores:
        copy.wait()


def parts_kernel(
    out_in, grad_in, par_in, out_to, grad_to, mw_to, mb_to, nw_to, nb_to, out, grad, par, mb, nb, sem
):
    moves = [(out_in, out, out_to), (grad_in, grad, grad_to)]
    for level in range(3):
        at = 4 * W * level
        for first, to in ((at, mw_to), (at + 2 * W, nw_to)):
            rows = slice(first, first + 2 * W)
            moves.append((par_in.at[rows, :], par.at[rows, :], to.at[level]))
    tail = slice(12 * W, 12 * W + 16)
    bias = pltpu.make_async_copy(par_in.at[tail, :], par.at[tail, :], sem.at[16])
    bias.start()
    loads = [pltpu.make_async_copy(src, mid, sem.at[i]) for i, (src, mid, _) in enumerate(moves)]
    for copy in loads:
        copy.start()
    stores = [pltpu.make_async_copy(mid, dst, sem.at[8 + i]) for i, (_, mid, dst) in enumerate(moves)]
    bias.wait()
    f_bias, a_bias = par[12 * W : 12 * W + 8, :], par[12 * W + 8 :, :]
    mb[...] = jnp.concatenate([f_bias[0:1], a_bias[0:1], a_bias[2:3]], axis=0)
    nb[...] = jnp.concatenate([f_bias[1:2], a_bias[1:2], a_bias[3:4]], axis=0)
    stores.append(pltpu.make_async_copy(mb, mb_to, sem.at[17]))
    stores.append(pltpu.make_async_copy(nb, nb_to, sem.at[18]))
    stores[8].start()
    stores[9].start()
    for load, store in zip(loads, stores):
        load.wait()
        store.start()
    for copy in stores:
        copy.wait()


def one_step(split, packed, *args):
    (fine_nodes, cotangent, msg_weights, msg_biases, node_weights, node_biases, node_count,
     fine_edges, fine_send, pool_map, coarse_edges, top_map, top_edges) = args
    Z, Y, C = split
    X = lax.axis_size("grp")
    NP = X * Z * Y * C
    nf = fine_nodes.shape[0]
    ne, nec, et = fine_edges.shape[2], coarse_edges.shape[2], top_edges.shape[1]
    nc = top_map.shape[1]
    vm = lambda *shape: pltpu.VMEM(shape, F32)
    vb = lambda *shape: pltpu.VMEM(shape, BF)
    ext_n = nf + 128
    gathers = [vm(Z * C, ROWS, W), vb(2, X * Y, Z * C * ROWS // 2, W)]

    def reduce_bufs(total):
        r = total // 2 // X // Y
        return [
            vm(2, total // 2 + ROWS, W),
            vm(total // 2 + ROWS, W),
            vm(X * Y, r + ROWS, W),
            vm(X * Y, r + ROWS, W),
            vm(Z, r + ROWS, W),
            vm(2, X * Y, r, W),
        ]

    loaded = args[:6] + args[7:]
    outs = [
        jax.ShapeDtypeStruct((nf, W), BF),
        jax.ShapeDtypeStruct((nf, W), F32),
        jax.ShapeDtypeStruct((12 * W + 16, W), F32),
    ]
    scratch = [pltpu.VMEM(a.shape, a.dtype) for a in [*loaded, *outs]]
    scratch += [
        pltpu.SemaphoreType.DMA((15,)),
        vm(4, TILE, W), vb(TILE, 2 * W),
        vb(ne, ext_n + nf), vb(ext_n + nf, ne), vb(ext_n + nf, 2 * W), vm(ne, W), vb(ne, 2 * W),
        vm(nf, W), vb(nf, W), vb(nf, W), vb(TILE, nf), vb(nf, TILE),
        vb(nec, 2 * TILE), vb(2 * TILE, nec), vb(2 * TILE, NP * ROWS), vb(2 * TILE, TILE),
        vb(2 * TILE, TILE), pltpu.VMEM((2 * TILE, TILE), I32), vm(TILE, TILE), vm(TILE, TILE),
        vb(128, W), vb(128, W), vm(2 * nc + 8, W), vm(2 * nc + 8, W), vm(nc, W), vm(nc, W),
        vm(8, W), vm(8, W), vm(2, 16, W), vm(2, 16, W),
        vm(nc + 8, W), vm(nc + 8, W), vm(8, W), vm(8, W), vm(8, W), vm(8, W),
        vm(2, 8, W), vm(2, 8, W),
        *gathers, *gathers,
        vm(8, W), vm(2, 8, W), vb(nc, W), vb(nc, W), vm(8, W), vm(2, 8, W),
        vm(nc + 8, W), vm(nc + 8, W), vm(8, W), vm(8, W), vm(8, W), vb(128, W), vb(128, W),
        *reduce_bufs(4 * W), *reduce_bufs(8 * W),
    ]
    copies = 24 + 2 * (X * Y + Z * C) + 2 * (2 * X * Y + Z)
    scratch += [pltpu.SemaphoreType.DMA((copies,)), pltpu.SemaphoreType.DMA((copies,))]
    in_hbm = pl.BlockSpec(memory_space=pltpu.HBM)
    sizes = (X, Z, Y, C, nf, ne, nc, nec, et // TILE)
    return pl.pallas_call(
        functools.partial(step_kernel, sizes, packed),
        out_shape=outs,
        in_specs=[in_hbm] * 6 + [pl.BlockSpec(memory_space=pltpu.SMEM)] + [in_hbm] * 6,
        out_specs=[in_hbm] * 3,
        scratch_shapes=scratch,
        compiler_params=pltpu.CompilerParams(
            collective_id=0 if packed else 1, has_side_effects=True, vmem_limit_bytes=64 * 1024 * 1024
        ),
        name="step" if packed else "step_long",
    )(*args)


def per_device(split, *args):
    owner = args[-1] // ROWS
    digits = jnp.arange(16)[None, :, None]
    high = (owner[:, None, :] // 16 == digits).astype(BF)
    low = (owner[:, None, :] % 16 == digits).astype(BF)
    counts = jnp.einsum("khe,kle->khl", high, low, preferred_element_type=F32)
    outs = lax.cond(
        jnp.max(counts) <= CAP,
        functools.partial(one_step, split, True),
        functools.partial(one_step, split, False),
        *args,
    )
    in_hbm = pl.BlockSpec(memory_space=pltpu.HBM)
    like = [outs[0], outs[1], args[2], args[3], args[4], args[5]]
    types = [BF, F32, F32, F32, F32, F32]
    return tuple(
        pl.pallas_call(
            parts_kernel,
            out_shape=[jax.ShapeDtypeStruct(a.shape, t) for a, t in zip(like, types)],
            in_specs=[in_hbm] * 3,
            out_specs=[in_hbm] * 6,
            scratch_shapes=[
                *[pltpu.VMEM(a.shape, a.dtype) for a in outs],
                pltpu.VMEM((3, W), F32),
                pltpu.VMEM((3, W), F32),
                pltpu.SemaphoreType.DMA((19,)),
            ],
            name="parts",
        )(*outs)
    )


def solution(mesh):
    return jax.shard_map(
        functools.partial(per_device, DOM_SPLIT),
        mesh=mesh,
        in_specs=(
            P(("grp", "dom"), None),
            P(("grp", "dom"), None),
            P(),
            P(),
            P(),
            P(),
            P(("grp", "dom")),
            P(("grp", "dom"), None, None),
            P(("grp", "dom"), None, None),
            P(("grp", "dom"), None),
            P(("grp", "dom"), None, None),
            P(("grp", "dom"), None),
            P(),
        ),
        out_specs=(P(("grp", "dom"), None), P(("grp", "dom"), None), P(), P(), P(), P()),
        check_vma=False,
    )
```

```python
import functools

import jax
import jax.numpy as jnp
from jax import lax
from jax.experimental import pallas as pl
from jax.experimental.pallas import tpu as pltpu
from jax.sharding import PartitionSpec as P

BF, F32, I32, I16 = jnp.bfloat16, jnp.float32, jnp.int32, jnp.int16
MESH = pl.DeviceIdType.MESH
W = 128
TILE = 128
CAP = 128
DOM_SPLIT = (8, 4, 2)
ROWS = 8


def mm(a, b):
    return jnp.dot(a, b, preferred_element_type=F32)


def nt(a, b):
    return lax.dot_general(a, b, (((1,), (1,)), ((), ())), preferred_element_type=F32)


def tn(a, b):
    return lax.dot_general(a, b, (((0,), (0,)), ((), ())), preferred_element_type=F32)


def wide(v):
    high = v.astype(BF)
    return jnp.concatenate([high, (v - high.astype(F32)).astype(BF)], axis=1)


def fold(v):
    return v[:, :W] + v[:, W:]


def nt_split(v, weight):
    high = v.astype(BF)
    return nt(high, weight) + nt((v - high.astype(F32)).astype(BF), weight)


def iota(shape, dim):
    return lax.broadcasted_iota(I32, shape, dim)


def hot(mask):
    return jnp.where(mask, 1.0, 0.0).astype(BF)


def hot16(mask):
    return jnp.where(mask, jnp.ones(mask.shape, BF), jnp.zeros(mask.shape, BF))


def down_lanes(row):
    return jnp.transpose(jnp.broadcast_to(row, (TILE, TILE)))


def sigmoid(v):
    return 0.5 * jnp.tanh(0.5 * v) + 0.5


def pad_rows(v, total=TILE):
    return jnp.concatenate([v, jnp.zeros((total - v.shape[0], v.shape[1]), v.dtype)], axis=0)


def sum_slots(ref, count):
    total = ref[0]
    for slot in range(1, count):
        total = total + ref[slot]
    return total


def step_kernel(
    sizes, packed,
    x_in, cot_in, mw_in, mb_in, nw_in, nb_in, cnt_ref, fe_in, fs_in, pm_in, ce_in, tm_in, te_in,
    out_to, ngrad_to, par_to,
    x_ref, cot_ref, mw_ref, mb_ref, nw_ref, nb_ref, fe_ref, fs_ref, pm_ref, ce_ref, tm_ref, te_ref,
    out_ref, ngrad_ref, par_ref, lsem,
    sums_r, kept, gat, sca, hl, slope, msgs, act_slope, hidden, aggf, pool_t, pool_l,
    gcat, gcat_t, o_top, l_top, sc_top, te_s, pos_s, key_s,
    sendbuf, halo, lfs, lfr, e0s, e0r, e0d, e0dr, e0u, e0ur, e1s, e1r, pss, psr, psd, psdr, psu, psur, tss, tsr,
    cb1, tab1, cb2, tab2, ths, thr, cfs, cfr, gts, gtr, rgs, rgr, rus, rur, rdr, bgs, bgr,
    f_cs, f_cr, f_xs, f_xr, f_zr, f_g,
    a_cs, a_cr, a_xs, a_xr, a_zr, a_g,
    ssem, rsem,
):
    X, Z, Y, C, nf, ne, nc, nec, nrow = sizes
    DOM = Z * Y * C
    NP = X * DOM
    halo_n = 64
    ext_n = nf + 2 * halo_n
    rim = nc // 8
    gx = lax.axis_index("grp")
    dm = lax.axis_index("dom")
    p = gx * DOM + dm
    z = lax.div(dm, Y * C)
    y = lax.rem(lax.div(dm, C), Y)
    c = lax.rem(dm, C)
    xz = gx * Z + z
    up = lax.rem(p + 1, NP)
    dn = lax.rem(p + NP - 1, NP)
    has_dn = p > 0
    has_up = p < NP - 1
    up2 = lax.rem(p + 2, NP)
    dn2 = lax.rem(p + NP - 2, NP)
    has_dn2 = p > 1
    has_up2 = p < NP - 2
    XY = X * Y
    ZC = Z * C
    xy = gx * Y + y
    zc = z * C + c

    def spot_of(q):
        return (lax.div(q, DOM), lax.rem(q, DOM))

    def plane(q):
        return (lax.div(q, Y), z * (Y * C) + lax.rem(q, Y) * C + c)

    def column(q):
        return (gx, lax.div(q, C) * (Y * C) + y * C + lax.rem(q, C))

    up_dev, dn_dev, up2_dev, dn2_dev = spot_of(up), spot_of(dn), spot_of(up2), spot_of(dn2)
    core_dev = (gx, dm + 1 - 2 * c)
    plane_devs = [plane(lax.rem(xy + d, XY)) for d in range(1, XY)]
    column_devs = [column(lax.rem(zc + d, ZC)) for d in range(1, ZC)]
    z_devs = [column(lax.rem(zc + d * C, ZC)) for d in range(1, Z)]

    loads = {}
    for spot, (name, src, dst) in enumerate(
        (
            ("fs", fs_in, fs_ref), ("x", x_in, x_ref), ("pm", pm_in, pm_ref), ("cot", cot_in, cot_ref),
            ("tm", tm_in, tm_ref), ("fe", fe_in, fe_ref), ("mw", mw_in, mw_ref), ("mb", mb_in, mb_ref),
            ("ce", ce_in, ce_ref), ("te", te_in, te_ref), ("nw", nw_in, nw_ref), ("nb", nb_in, nb_ref),
        )
    ):
        loads[name] = pltpu.make_async_copy(src, dst, lsem.at[spot])
        loads[name].start()
    barrier = pltpu.get_barrier_semaphore()
    partners = [up_dev, dn_dev, up2_dev, dn2_dev] + plane_devs + column_devs
    for dev in partners:
        pl.semaphore_signal(barrier, inc=1, device_id=dev, device_id_type=MESH)

    started = []

    def send(src, dst, dev):
        spot = len(started)
        copy = pltpu.make_async_remote_copy(
            src_ref=src, dst_ref=dst, send_sem=ssem.at[spot], recv_sem=rsem.at[spot],
            device_id=dev, device_id_type=MESH,
        )
        copy.start()
        started.append(copy)
        return copy

    def arrived(copies):
        for copy in copies:
            copy.wait_recv()

    ntile = ne // TILE
    ctile = nec // TILE
    lane = iota((TILE, TILE), 1)
    sub = iota((TILE, TILE), 0)
    ones = jnp.ones((TILE, TILE), BF)

    loads["fs"].wait()
    loads["x"].wait()
    send_row = jnp.concatenate([fs_ref[0, 0:1, :], fs_ref[0, 1:2, :]], axis=1)
    send_lanes = down_lanes(send_row)
    picks = jnp.concatenate([hot(send_lanes == lane + g * TILE) for g in range(nf // TILE)], axis=1)
    sendbuf[...] = mm(picks, x_ref[...]).astype(BF)
    pl.semaphore_wait(barrier, len(partners))
    halo_in = [
        send(sendbuf.at[halo_n : 2 * halo_n], halo.at[0:halo_n], up_dev),
        send(sendbuf.at[0:halo_n], halo.at[halo_n : 2 * halo_n], dn_dev),
    ]

    loads["pm"].wait()
    loads["tm"].wait()
    live = cnt_ref[0]
    alive = jnp.where(iota((nf, W), 0) < live, 1.0, 0.0)
    for g in range(nf // TILE):
        keys = pm_ref[0:1, g * TILE : (g + 1) * TILE]
        pool_t[:, g * TILE : (g + 1) * TILE] = hot((sub == keys) & (lane + g * TILE < live))
    counts = mm(pool_t[...], jnp.ones((nf, W), BF))
    e0s[...] = jnp.concatenate([counts[nc:], counts[nc - rim : nc]], axis=0)
    e0d[...] = counts[:nc]
    e0u[...] = counts[2 * nc - rim :]
    rel = lax.rem(tm_ref[...] - (p - 1) * ROWS + NP * ROWS, NP * ROWS)
    rel = jnp.concatenate([rel, jnp.full((1, TILE - nc), -1, I32)], axis=1)
    top_t = hot(sub == rel)
    top_counts = mm(top_t, ones)
    e1s[0, 0:ROWS, :] = top_counts[0:ROWS]
    e1s[1, 0:ROWS, :] = top_counts[2 * ROWS : 3 * ROWS]
    e0_in = [
        send(e0s, e0r, up_dev),
        send(e0d, e0dr, dn_dev),
        send(e0u, e0ur, up2_dev),
        send(e1s.at[0, 0:ROWS], e1r.at[0, 0:ROWS], dn_dev),
        send(e1s.at[1, 0:ROWS], e1r.at[1, 0:ROWS], up_dev),
    ]

    loads["fe"].wait()

    lane16, sub16 = lane.astype(I16), sub.astype(I16)

    def build(k, carry):
        at = pl.ds(pl.multiple_of(k * TILE, TILE), TILE)
        src, tgt = fe_ref[0, 0:1, at], fe_ref[0, 1:2, at]
        src_lanes, tgt_lanes = down_lanes(src).astype(I16), down_lanes(tgt).astype(I16)
        src16 = jnp.broadcast_to(src, (TILE, TILE)).astype(I16)
        tgt16 = jnp.broadcast_to(tgt, (TILE, TILE)).astype(I16)
        for g in range(ext_n // TILE):
            gat[at, g * TILE : (g + 1) * TILE] = hot16(src_lanes == lane16 + g * TILE)
            sca[g * TILE : (g + 1) * TILE, at] = hot16(sub16 == (src16 - g * TILE))
        for g in range(nf // TILE):
            gat[at, ext_n + g * TILE : ext_n + (g + 1) * TILE] = hot16(tgt_lanes == lane16 + g * TILE)
            sca[ext_n + g * TILE : ext_n + (g + 1) * TILE, at] = hot16(sub16 == (tgt16 - g * TILE))
        return carry

    lax.fori_loop(0, ntile, build, 0)
    loads["mw"].wait()
    loads["mb"].wait()
    ws0, wt0 = mw_ref[0, :W, :], mw_ref[0, W:, :]
    hl[0:nf, :] = wide(mm(x_ref[...], ws0))
    hl[ext_n : ext_n + nf, :] = wide(mm(x_ref[...], wt0) + mb_ref[0:1, :])

    arrived(halo_in)
    halo_rows = sub
    live_halo = (has_dn & (halo_rows < halo_n)) | (has_up & (halo_rows >= halo_n))
    halo_f = jnp.where(live_halo, halo[...].astype(F32), 0.0).astype(BF)
    hl[nf:ext_n, :] = wide(mm(halo_f, ws0))
    step = 4 * TILE

    def forward(k, carry):
        at = pl.ds(pl.multiple_of(k * step, step), step)
        pre = fold(mm(gat[at, :], hl[...]))
        s = sigmoid(pre)
        slope[at, :] = s * (1.0 + pre * (1.0 - s))
        msgs[at, :] = wide(pre * s)
        return carry

    lax.fori_loop(0, ne // step, forward, 0)

    loads["nw"].wait()
    loads["nb"].wait()

    def node_forward(rows, agg, level):
        act = mm(rows, nw_ref[level, :W, :]) + mm(agg, nw_ref[level, W:, :]) + nb_ref[level : level + 1, :]
        s = sigmoid(act)
        return (rows.astype(F32) + act * s).astype(BF), s * (1.0 + act * (1.0 - s))

    def node_backward(rows, agg, act_slopes, grad, level):
        g_act = grad * act_slopes
        low = g_act.astype(BF)
        pair = nt(low, nw_ref[level])
        return (
            grad + pair[:, :W],
            pair[:, W:].astype(BF),
            tn(rows, low),
            tn(agg, low),
            jnp.sum(g_act, axis=0, keepdims=True),
        )

    for k in range(nf // step):
        at = slice(k * step, (k + 1) * step)
        agg = fold(mm(sca[ext_n + k * step : ext_n + (k + 1) * step, :], msgs[...])).astype(BF)
        new, act_s = node_forward(x_ref[at, :], agg, 0)
        aggf[at, :] = agg
        hidden[at, :] = new
        act_slope[at, :] = act_s

    pooled = mm(pool_t[...], hidden[...])
    pss[...] = pooled[nc - rim :]
    psd[...] = pooled[:rim]
    psu[...] = pooled[2 * nc - rim :]
    ps_in = [send(pss, psr, up_dev), send(psd, psdr, dn_dev), send(psu, psur, up2_dev)]
    loads["ce"].wait()
    for k in range(ctile):
        src = ce_ref[0, 0:1, k * TILE : (k + 1) * TILE]
        tgt = ce_ref[0, 1:2, k * TILE : (k + 1) * TILE]
        gcat[k * TILE : (k + 1) * TILE, 0:TILE] = hot(down_lanes(src) == lane)
        gcat[k * TILE : (k + 1) * TILE, TILE:] = hot(down_lanes(tgt) == lane)
        gcat_t[0:TILE, k * TILE : (k + 1) * TILE] = hot(sub == src)
        gcat_t[TILE:, k * TILE : (k + 1) * TILE] = hot(sub == tgt)

    arrived(e0_in)
    lower_counts = jnp.where(has_dn, e0r[0:nc, :], 0.0)
    den = jnp.maximum(counts[:nc] + lower_counts, 1.0)
    den_up = jnp.maximum(e0dr[...] + counts[nc:], 1.0)
    den_dn = jnp.maximum(e0r[nc:, :] + jnp.where(has_dn2, e0ur[...], 0.0), 1.0)
    own_win = slice(ROWS, 2 * ROWS)
    top_den = jnp.maximum(top_counts[own_win] + e1r[0, 0:ROWS, :] + e1r[1, 0:ROWS, :], 1.0)
    arrived(ps_in)
    start_f = ((pooled[:nc] + jnp.where(has_dn, psr[rim:, :], 0.0)) / den).astype(BF).astype(F32)
    left = (psr[0:rim, :] + jnp.where(has_dn2, psur[...], 0.0)) / den_dn
    right = (psdr[...] + pooled[nc : nc + rim]) / den_up[:rim]
    start_p = pad_rows(start_f).astype(BF)
    ws1, wt1 = mw_ref[1, :W, :], mw_ref[1, W:, :]
    near_part = wide(mm(start_p, wt1) + mb_ref[1:2, :])
    cext = pad_rows(
        jnp.concatenate(
            [jnp.where(has_dn, left, 0.0), start_f, jnp.where(has_up, right, 0.0)], axis=0
        )
    ).astype(BF)
    pre = fold(mm(gcat[...], jnp.concatenate([wide(mm(cext, ws1)), near_part], axis=0)))
    s = sigmoid(pre)
    slope_c = s * (1.0 + pre * (1.0 - s))
    agg_c = fold(mm(gcat_t[TILE:, :], wide(pre * s))).astype(BF)
    c_hidden, act_slope_c = node_forward(start_p, agg_c, 1)
    keep = sub < nc
    c_hidden_f = jnp.where(keep, c_hidden.astype(F32), 0.0)
    top_part = mm(top_t, c_hidden_f.astype(BF))
    tss[0] = top_part[0:ROWS]
    tss[1] = top_part[2 * ROWS : 3 * ROWS]
    ts_in = [send(tss.at[0], tsr.at[0], dn_dev), send(tss.at[1], tsr.at[1], up_dev)]
    first = p * ROWS

    def owned(values):
        return (values >= first) & (values < first + ROWS)

    def keys_of(src, tgt):
        return (src * (NP * ROWS) + tgt + 1).astype(F32)

    def ends(key):
        code = key.astype(I32) - 1
        empty = code < 0
        return (
            jnp.where(empty, -1, lax.div(code, NP * ROWS)),
            jnp.where(empty, -1, lax.rem(code, NP * ROWS)),
        )

    def place(node):
        part = lax.div(node, ROWS)
        core = lax.rem(part, C)
        py = lax.rem(lax.div(part, C), Y)
        pz = lax.rem(lax.div(part, C * Y), Z)
        px = lax.div(part, C * Y * Z)
        inner = (pz * C + core) * ROWS + lax.rem(node, ROWS)
        spot = lax.div(inner, half) * (XY * half) + (px * Y + py) * half + lax.rem(inner, half)
        return jnp.where(node < 0, -1, spot)

    half = ZC * ROWS // 2
    near = jnp.where(lane < ROWS, lane + first, -2)
    near_t = jnp.where(sub < ROWS, sub + first, -2)

    def fill(t_lanes, s_lanes):
        (t_src, t_tgt), (s_src, s_tgt) = ends(t_lanes), ends(s_lanes)
        t_far, s_far = place(t_src), place(s_tgt)
        for g in range(NP * ROWS // TILE):
            o_top[0:TILE, g * TILE : (g + 1) * TILE] = hot(t_far == lane + g * TILE)
            o_top[TILE:, g * TILE : (g + 1) * TILE] = hot(s_far == lane + g * TILE)
        l_top[0:TILE, :] = hot(t_tgt == near)
        l_top[TILE:, :] = hot(s_src == near)
        sc_top[0:TILE, :] = hot(ends(jnp.transpose(t_lanes))[1] == near_t)
        sc_top[TILE:, :] = hot(ends(jnp.transpose(s_lanes))[0] == near_t)

    def fill_row(r):
        src, tgt = te_s[pl.ds(r, 1), :], te_s[pl.ds(TILE + r, 1), :]
        key = keys_of(src, tgt)
        fill(
            down_lanes(jnp.where(owned(tgt), key, 0.0)), down_lanes(jnp.where(owned(src), key, 0.0))
        )

    loads["te"].wait()
    te_s[...] = jnp.full(te_s.shape, -1, I32)

    def lay(r, carry):
        at = pl.ds(pl.multiple_of(r * TILE, TILE), TILE)
        te_s[pl.ds(r, 1), :] = te_ref[0:1, at]
        te_s[pl.ds(TILE + r, 1), :] = te_ref[1:2, at]
        return carry

    lax.fori_loop(0, nrow, lay, 0)

    if packed:
        upper_ones = hot(sub <= lane)
        lower_ones = hot(lane < sub)
        sub_f = sub.astype(F32)
        key_s[...] = keys_of(te_s[0:TILE, :], te_s[TILE:, :])
        lists = []
        for values in (te_s[TILE:, :], te_s[0:TILE, :]):
            mine = owned(values)
            flags = hot(mine)
            offset = mm(lower_ones, mm(flags, ones).astype(BF))
            pos_s[...] = jnp.where(mine, mm(flags, upper_ones) + offset - 1.0, -1.0)

            def pick(r, acc):
                at = pl.ds(pl.multiple_of(r * 8, 8), 8)
                places, keys8 = pos_s[at, :], key_s[at, :]
                for i in range(8):
                    acc = acc + jnp.where(places[i : i + 1, :] == sub_f, keys8[i : i + 1, :], 0.0)
                return acc

            acc = lax.fori_loop(0, -(-nrow // 8), pick, jnp.zeros((TILE, TILE), F32))
            lists.append(jnp.broadcast_to(jnp.sum(acc, axis=1, keepdims=True), (TILE, TILE)))
    arrived(ts_in)
    top_start = ((top_part[own_win] + tsr[0] + tsr[1]) / top_den).astype(BF)

    def gather(own, cb, tab):
        cb[zc] = own
        copies = [send(cb.at[zc], cb.at[zc], dev) for dev in column_devs]
        yield
        arrived(copies)
        tab[c, xy] = cb[pl.ds(c * (ZC // 2), ZC // 2)].reshape(half, W).astype(BF)
        copies = [send(tab.at[c, xy], tab.at[c, xy], dev) for dev in plane_devs]
        yield
        arrived(copies)
        copies = [send(tab.at[c], tab.at[c], core_dev)]
        yield
        arrived(copies)

    first_gather = gather(top_start.astype(F32), cb1, tab1)
    next(first_gather)
    if packed:
        fill(*lists)

    next(first_gather)

    loads["cot"].wait()
    gout = cot_ref[...] * alive
    lift = fold(mm(pool_t[...], wide(gout)))
    lfs[...] = lift[nc:]
    lf_in = [send(lfs, lfr, up_dev)]
    top_l = hot(down_lanes(rel) == lane)
    for g in range(nf // TILE):
        keys = pm_ref[0:1, g * TILE : (g + 1) * TILE]
        pool_l[g * TILE : (g + 1) * TILE, :] = hot((down_lanes(keys) == lane) & (sub + g * TILE < live))
    next(first_gather)
    arrived(lf_in)
    grad_coarse0 = lift[:nc] + jnp.where(has_dn, lfr[...], 0.0)
    top_g = fold(mm(top_t, pad_rows(wide(grad_coarse0))))
    e1s[0, ROWS:, :] = top_g[0:ROWS]
    e1s[1, ROWS:, :] = top_g[2 * ROWS : 3 * ROWS]
    e1_in = [
        send(e1s.at[0, ROWS:], e1r.at[0, ROWS:], dn_dev),
        send(e1s.at[1, ROWS:], e1r.at[1, ROWS:], up_dev),
    ]
    for _ in first_gather:
        pass

    ws2, wt2, mb2 = mw_ref[2, :W, :], mw_ref[2, W:, :], mb_ref[2:3, :]
    top_rows = pad_rows(top_start.astype(F32)).astype(BF)
    kept[:, 0:W] = top_rows

    def t_edges():
        far = mm(o_top[0:TILE, :], tab1[...].reshape(NP * ROWS, W)).astype(BF)
        close = mm(l_top[0:TILE, :], kept[:, 0:W]).astype(BF)
        pre_t = mm(far, ws2) + mm(close, wt2) + mb2
        s = sigmoid(pre_t)
        return far, close, pre_t * s, s * (1.0 + pre_t * (1.0 - s))

    def t_sums(message):
        return fold(mm(sc_top[0:TILE, :], wide(message)))

    def t_back(far, close, slope_t):
        g_pre_t = mm(l_top[0:TILE, :], kept[:, W:]) * slope_t
        low_t = g_pre_t.astype(BF)
        return (
            tn(far, low_t),
            tn(close, low_t),
            mm(sc_top[0:TILE, :], low_t),
            jnp.sum(g_pre_t, axis=0, keepdims=True),
        )

    def s_slopes():
        far = mm(o_top[TILE:, :], tab1[...].reshape(NP * ROWS, W)).astype(BF)
        close = mm(l_top[TILE:, :], kept[:, 0:W]).astype(BF)
        pre_s = mm(close, ws2) + mm(far, wt2) + mb2
        s = sigmoid(pre_s)
        return s * (1.0 + pre_s * (1.0 - s))

    def s_back(slope_s):
        g_far = mm(o_top[TILE:, :], tab2[...].reshape(NP * ROWS, W))
        return mm(sc_top[TILE:, :], (g_far * slope_s).astype(BF))

    def over_rows(work):
        sums_r[...] = jnp.zeros(sums_r.shape, F32)

        def one(r, carry):
            fill_row(r)
            for spot, term in enumerate(work()):
                sums_r[spot, 0 : term.shape[0], :] += term
            return carry

        lax.fori_loop(0, nrow, one, 0)

    def t_back_row():
        far = mm(o_top[0:TILE, :], tab1[...].reshape(NP * ROWS, W)).astype(BF)
        both = mm(l_top[0:TILE, :], kept[...])
        close = both[:, 0:W].astype(BF)
        pre_t = mm(far, ws2) + mm(close, wt2) + mb2
        s = sigmoid(pre_t)
        g_pre_t = both[:, W:] * (s * (1.0 + pre_t * (1.0 - s)))
        low_t = g_pre_t.astype(BF)
        return (
            tn(far, low_t),
            tn(close, low_t),
            mm(sc_top[0:TILE, :], low_t),
            jnp.sum(g_pre_t, axis=0, keepdims=True),
        )

    if packed:
        t_far_rows, t_close_rows, message, slope_t = t_edges()
        agg_t = t_sums(message).astype(BF)
    else:
        over_rows(lambda: (t_sums(t_edges()[2]),))
        agg_t = sums_r[0].astype(BF)
    t_hidden, act_slope_t = node_forward(top_rows, agg_t, 2)
    arrived(e1_in)
    top_grad = pad_rows(top_g[own_win] + e1r[0, ROWS:, :] + e1r[1, ROWS:, :])
    g_nodes, g_agg, dwn2_a, dwn2_b, dbn2 = node_backward(top_rows, agg_t, act_slope_t, top_grad, 2)
    kept[:, W:] = g_agg
    key_s[...] = g_nodes
    a_cs[1, 2 * W : 3 * W, :] = dwn2_a
    a_cs[1, 3 * W : 4 * W, :] = dwn2_b
    second = gather(g_agg.astype(F32)[:ROWS], cb2, tab2)
    next(second)
    own_hidden = t_hidden.astype(F32)[:ROWS]
    ths[...] = own_hidden
    th_in = [send(ths, thr.at[0], dn_dev), send(ths, thr.at[1], up_dev)]
    if packed:
        slope_s = s_slopes()
        backs = t_back(t_far_rows, t_close_rows, slope_t)
    else:
        over_rows(t_back_row)
        backs = sums_r[0], sums_r[1], sums_r[2], sums_r[3, 0:1, :]
    dwm2_a, dwm2_b, sums_t, dbm2 = backs
    a_half = a_cs.shape[1] - ROWS
    a_cs[1, 0:W, :] = dwm2_a
    a_cs[1, W : 2 * W, :] = dwm2_b
    g_nodes = key_s[...] + nt_split(sums_t, wt2)
    next(second)
    arrived(th_in)
    window = pad_rows(jnp.concatenate([thr[1], own_hidden, thr[0]], axis=0)).astype(BF)
    final = (c_hidden_f + mm(top_l, window)).astype(BF)[:nc]
    cfs[...] = final
    cf_in = [send(cfs, cfr, dn_dev)]
    arrived(cf_in)
    lift_rows = jnp.concatenate([final, cfr[...]], axis=0)
    lifted = mm(pool_l[...], lift_rows)
    out_ref[...] = ((hidden[...].astype(F32) + lifted) * alive).astype(BF)
    stores = [pltpu.make_async_copy(out_ref, out_to, lsem.at[12])]
    stores[0].start()
    for _ in second:
        pass

    if packed:
        sums_s = s_back(slope_s)
    else:
        over_rows(lambda: (s_back(s_slopes()),))
        sums_s = sums_r[0]
    g_nodes = g_nodes + nt_split(sums_s, ws2)
    g_own = g_nodes[:ROWS] / top_den
    gts[...] = g_own
    gt_in = [send(gts, gtr.at[0], dn_dev), send(gts, gtr.at[1], up_dev)]
    arrived(gt_in)
    window = pad_rows(jnp.concatenate([gtr[1], g_own, gtr[0]], axis=0))
    grad_coarse = pad_rows(grad_coarse0) + fold(mm(top_l, wide(window)))

    g_nodes, g_agg, dwn1_a, dwn1_b, dbn1 = node_backward(start_p, agg_c, act_slope_c, grad_coarse, 1)
    g_pre = mm(gcat[:, TILE:], g_agg) * slope_c
    dbm1 = jnp.sum(g_pre, axis=0, keepdims=True)
    sums = mm(gcat_t[...], g_pre.astype(BF))
    g_ext = nt_split(sums[:TILE], ws1)
    g_start = (g_nodes + nt_split(sums[TILE:], wt1))[:nc] + g_ext[rim : rim + nc]
    rgs[0:nc, :] = g_start
    rgs[nc:, :] = g_ext[:rim]
    rus[...] = g_ext[rim + nc : 2 * rim + nc]
    rg_in = [
        send(rgs, rgr, dn_dev),
        send(rus, rur, up_dev),
        send(rgs.at[nc : nc + rim], rdr, dn2_dev),
    ]
    a_cs[0, 0:W, :] = fold(tn(cext, wide(sums[:TILE])))
    a_cs[0, W : 2 * W, :] = fold(tn(start_p, wide(sums[TILE:])))
    a_cs[0, 2 * W : 3 * W, :] = dwn1_a
    a_cs[0, 3 * W : 4 * W, :] = dwn1_b
    a_bias = jnp.concatenate([dbm1, dbn1, dbm2, dbn2, jnp.zeros((4, W), F32)], axis=0)
    a_cs[0, a_half:, :] = a_bias
    a_cs[1, a_half:, :] = a_bias

    scale = 1.0 / float(nf * NP) ** 0.5

    def reduce(cs, cr, xs, xr, zr, g, biases):
        copies = [send(cs.at[1 - c], cr, core_dev)]
        yield
        arrived(copies)
        part = cs[c] + cr[...]
        n = g.shape[2]
        for j in range(XY):
            xs[j, 0:n, :] = part[j * n : (j + 1) * n]
            xs[j, n:, :] = part[XY * n :]
        copies = [
            send(xs.at[lax.rem(xy + d + 1, XY)], xr.at[xy], dev) for d, dev in enumerate(plane_devs)
        ]
        xr[xy] = xs[xy]
        yield
        arrived(copies)
        zr[z] = sum_slots(xr, XY)
        copies = [send(zr.at[z], zr.at[z], dev) for dev in z_devs]
        yield
        arrived(copies)
        part = sum_slots(zr, Z) * scale
        biases.append(part[n:])
        g[c, xy] = part[:n]
        copies = [send(g.at[c, xy], g.at[c, xy], dev) for dev in plane_devs]
        yield
        arrived(copies)
        copies = [send(g.at[c], g.at[c], core_dev)]
        yield
        arrived(copies)

    a_bias_out, f_bias_out = [], []
    reduce_a = reduce(a_cs, a_cr, a_xs, a_xr, a_zr, a_g, a_bias_out)
    next(reduce_a)
    arrived(rg_in)
    middle = jnp.zeros((nc - 2 * rim, W), F32)
    g_csum = (
        g_start
        + jnp.concatenate(
            [jnp.where(has_dn, rur[...], 0.0), middle, jnp.where(has_up, rgr[nc:, :], 0.0)], axis=0
        )
    ) / den
    upper = (
        rgr[0:nc, :] + jnp.concatenate([rus[...], middle, jnp.where(has_up2, rdr[...], 0.0)], axis=0)
    ) / den_up
    pool_grad = jnp.concatenate([g_csum, jnp.where(has_up, upper, 0.0)], axis=0)
    grad_fine = gout + fold(mm(pool_l[...], wide(pool_grad)))

    g_nodes, g_agg, dwn0_a, dwn0_b, dbn0 = node_backward(x_ref[...], aggf[...], act_slope[...], grad_fine, 0)
    aggf[...] = g_agg
    f_cs[1, 0:W, :] = dwn0_a
    f_cs[1, W : 2 * W, :] = dwn0_b

    def backward(k, total):
        at = pl.ds(pl.multiple_of(k * step, step), step)
        g_pre = mm(gat[at, ext_n:], aggf[...]) * slope[at, :]
        msgs[at, 0:W] = g_pre.astype(BF)
        return total + jnp.sum(g_pre, axis=0, keepdims=True)

    dbm0 = lax.fori_loop(0, ne // step, backward, jnp.zeros((1, W), F32))
    sums_h = mm(sca[nf:ext_n, :], msgs[:, 0:W])
    bgs[...] = nt_split(sums_h, ws0).astype(BF)
    bg_in = [
        send(bgs.at[0:halo_n], bgr.at[halo_n : 2 * halo_n], dn_dev),
        send(bgs.at[halo_n : 2 * halo_n], bgr.at[0:halo_n], up_dev),
    ]
    sums_s = mm(sca[0:nf, :], msgs[:, 0:W])
    sums_t = mm(sca[ext_n:, :], msgs[:, 0:W])
    f_cs[0, 0:W, :] = fold(tn(x_ref[...], wide(sums_s)) + tn(halo_f, wide(sums_h)))
    f_cs[0, W : 2 * W, :] = fold(tn(x_ref[...], wide(sums_t)))
    f_bias = jnp.concatenate([dbm0, dbn0, jnp.zeros((6, W), F32)], axis=0)
    f_half = f_cs.shape[1] - ROWS
    f_cs[0, f_half:, :] = f_bias
    f_cs[1, f_half:, :] = f_bias
    reduce_f = reduce(f_cs, f_cr, f_xs, f_xr, f_zr, f_g, f_bias_out)
    next(reduce_f)
    next(reduce_a)
    node_grad = g_nodes + nt_split(sums_s, ws0) + nt_split(sums_t, wt0)
    arrived(bg_in)
    live_back = (has_dn & (sub < halo_n)) | (has_up & (sub >= halo_n))
    back = jnp.where(live_back, bgr[...].astype(F32), 0.0).astype(BF)
    for g in range(nf // TILE):
        at = slice(g * TILE, (g + 1) * TILE)
        ngrad_ref[at, :] = node_grad[at] + mm(hot(sub + g * TILE == send_row), back)
    stores.append(pltpu.make_async_copy(ngrad_ref, ngrad_to, lsem.at[13]))
    stores[1].start()
    pending = [reduce_f, reduce_a]
    while pending:
        for item in list(pending):
            if next(item, 0) == 0:
                pending.remove(item)

    for copy in started:
        copy.wait_send()
    par_ref[0 : 4 * W, :] = f_g[...].reshape(4 * W, W)
    par_ref[4 * W : 12 * W, :] = a_g[...].reshape(8 * W, W)
    par_ref[12 * W : 12 * W + 8, :] = f_bias_out[0]
    par_ref[12 * W + 8 :, :] = a_bias_out[0]
    stores.append(pltpu.make_async_copy(par_ref, par_to, lsem.at[14]))
    stores[2].start()
    for copy in stores:
        copy.wait()


def parts_kernel(
    out_in, grad_in, par_in, out_to, grad_to, mw_to, mb_to, nw_to, nb_to, out, grad, par, mb, nb, sem
):
    moves = [(out_in, out, out_to), (grad_in, grad, grad_to)]
    for level in range(3):
        at = 4 * W * level
        for first, to in ((at, mw_to), (at + 2 * W, nw_to)):
            rows = slice(first, first + 2 * W)
            moves.append((par_in.at[rows, :], par.at[rows, :], to.at[level]))
    tail = slice(12 * W, 12 * W + 16)
    bias = pltpu.make_async_copy(par_in.at[tail, :], par.at[tail, :], sem.at[16])
    bias.start()
    loads = [pltpu.make_async_copy(src, mid, sem.at[i]) for i, (src, mid, _) in enumerate(moves)]
    for copy in loads:
        copy.start()
    stores = [pltpu.make_async_copy(mid, dst, sem.at[8 + i]) for i, (_, mid, dst) in enumerate(moves)]
    bias.wait()
    f_bias, a_bias = par[12 * W : 12 * W + 8, :], par[12 * W + 8 :, :]
    mb[...] = jnp.concatenate([f_bias[0:1], a_bias[0:1], a_bias[2:3]], axis=0)
    nb[...] = jnp.concatenate([f_bias[1:2], a_bias[1:2], a_bias[3:4]], axis=0)
    stores.append(pltpu.make_async_copy(mb, mb_to, sem.at[17]))
    stores.append(pltpu.make_async_copy(nb, nb_to, sem.at[18]))
    stores[8].start()
    stores[9].start()
    for load, store in zip(loads, stores):
        load.wait()
        store.start()
    for copy in stores:
        copy.wait()


def one_step(split, packed, *args):
    (fine_nodes, cotangent, msg_weights, msg_biases, node_weights, node_biases, node_count,
     fine_edges, fine_send, pool_map, coarse_edges, top_map, top_edges) = args
    Z, Y, C = split
    X = lax.axis_size("grp")
    NP = X * Z * Y * C
    nf = fine_nodes.shape[0]
    ne, nec, et = fine_edges.shape[2], coarse_edges.shape[2], top_edges.shape[1]
    nc = top_map.shape[1]
    vm = lambda *shape: pltpu.VMEM(shape, F32)
    vb = lambda *shape: pltpu.VMEM(shape, BF)
    ext_n = nf + 128
    gathers = [vm(Z * C, ROWS, W), vb(2, X * Y, Z * C * ROWS // 2, W)]

    def reduce_bufs(total):
        r = total // 2 // X // Y
        return [
            vm(2, total // 2 + ROWS, W),
            vm(total // 2 + ROWS, W),
            vm(X * Y, r + ROWS, W),
            vm(X * Y, r + ROWS, W),
            vm(Z, r + ROWS, W),
            vm(2, X * Y, r, W),
        ]

    loaded = args[:6] + args[7:]
    outs = [
        jax.ShapeDtypeStruct((nf, W), BF),
        jax.ShapeDtypeStruct((nf, W), F32),
        jax.ShapeDtypeStruct((12 * W + 16, W), F32),
    ]
    scratch = [pltpu.VMEM(a.shape, a.dtype) for a in [*loaded, *outs]]
    scratch += [
        pltpu.SemaphoreType.DMA((15,)),
        vm(4, TILE, W), vb(TILE, 2 * W),
        vb(ne, ext_n + nf), vb(ext_n + nf, ne), vb(ext_n + nf, 2 * W), vm(ne, W), vb(ne, 2 * W),
        vm(nf, W), vb(nf, W), vb(nf, W), vb(TILE, nf), vb(nf, TILE),
        vb(nec, 2 * TILE), vb(2 * TILE, nec), vb(2 * TILE, NP * ROWS), vb(2 * TILE, TILE),
        vb(2 * TILE, TILE), pltpu.VMEM((2 * TILE, TILE), I32), vm(TILE, TILE), vm(TILE, TILE),
        vb(128, W), vb(128, W), vm(nc, W), vm(nc, W), vm(nc + 8, W), vm(nc + 8, W), vm(nc, W), vm(nc, W),
        vm(8, W), vm(8, W), vm(2, 16, W), vm(2, 16, W),
        vm(nc + 8, W), vm(nc + 8, W), vm(8, W), vm(8, W), vm(8, W), vm(8, W),
        vm(2, 8, W), vm(2, 8, W),
        *gathers, *gathers,
        vm(8, W), vm(2, 8, W), vb(nc, W), vb(nc, W), vm(8, W), vm(2, 8, W),
        vm(nc + 8, W), vm(nc + 8, W), vm(8, W), vm(8, W), vm(8, W), vb(128, W), vb(128, W),
        *reduce_bufs(4 * W), *reduce_bufs(8 * W),
    ]
    copies = 28 + 2 * (X * Y + Z * C) + 2 * (2 * X * Y + Z)
    scratch += [pltpu.SemaphoreType.DMA((copies,)), pltpu.SemaphoreType.DMA((copies,))]
    in_hbm = pl.BlockSpec(memory_space=pltpu.HBM)
    sizes = (X, Z, Y, C, nf, ne, nc, nec, et // TILE)
    return pl.pallas_call(
        functools.partial(step_kernel, sizes, packed),
        out_shape=outs,
        in_specs=[in_hbm] * 6 + [pl.BlockSpec(memory_space=pltpu.SMEM)] + [in_hbm] * 6,
        out_specs=[in_hbm] * 3,
        scratch_shapes=scratch,
        compiler_params=pltpu.CompilerParams(
            collective_id=0 if packed else 1, has_side_effects=True, vmem_limit_bytes=64 * 1024 * 1024
        ),
        name="step" if packed else "step_long",
    )(*args)


def lists_kernel(te_in, fit_ref, te, sem):
    load = pltpu.make_async_copy(te_in, te, sem)
    load.start()
    load.wait()
    most = 0.0
    for end in range(2):
        owner = lax.div(te[end : end + 1, :], ROWS)
        digits = iota((16, te.shape[1]), 0)
        counts = nt(hot(lax.div(owner, 16) == digits), hot(lax.rem(owner, 16) == digits))
        most = jnp.maximum(most, jnp.max(counts))
    fit_ref[0] = (most <= CAP).astype(I32)


def per_device(split, *args):
    fit = pl.pallas_call(
        lists_kernel,
        out_shape=jax.ShapeDtypeStruct((1,), I32),
        in_specs=[pl.BlockSpec(memory_space=pltpu.HBM)],
        out_specs=pl.BlockSpec(memory_space=pltpu.SMEM),
        scratch_shapes=[pltpu.VMEM(args[-1].shape, I32), pltpu.SemaphoreType.DMA],
        name="lists",
    )(args[-1])
    outs = lax.cond(
        fit[0] > 0,
        functools.partial(one_step, split, True),
        functools.partial(one_step, split, False),
        *args,
    )
    in_hbm = pl.BlockSpec(memory_space=pltpu.HBM)
    like = [outs[0], outs[1], args[2], args[3], args[4], args[5]]
    types = [BF, F32, F32, F32, F32, F32]
    return tuple(
        pl.pallas_call(
            parts_kernel,
            out_shape=[jax.ShapeDtypeStruct(a.shape, t) for a, t in zip(like, types)],
            in_specs=[in_hbm] * 3,
            out_specs=[in_hbm] * 6,
            scratch_shapes=[
                *[pltpu.VMEM(a.shape, a.dtype) for a in outs],
                pltpu.VMEM((3, W), F32),
                pltpu.VMEM((3, W), F32),
                pltpu.SemaphoreType.DMA((19,)),
            ],
            name="parts",
        )(*outs)
    )


def solution(mesh):
    return jax.shard_map(
        functools.partial(per_device, DOM_SPLIT),
        mesh=mesh,
        in_specs=(
            P(("grp", "dom"), None),
            P(("grp", "dom"), None),
            P(),
            P(),
            P(),
            P(),
            P(("grp", "dom")),
            P(("grp", "dom"), None, None),
            P(("grp", "dom"), None, None),
            P(("grp", "dom"), None),
            P(("grp", "dom"), None, None),
            P(("grp", "dom"), None),
            P(),
        ),
        out_specs=(P(("grp", "dom"), None), P(("grp", "dom"), None), P(), P(), P(), P()),
        check_vma=False,
    )
```
